512 devices in a mesh: band: 4 (over x_hi, core), dom: 128 (over x_lo, z, y).
Axes of the slice: x: 4 (x_hi: 2, x_lo: 2; x = x_hi * 2 + x_lo), y: 8, z: 8, core: 2. Of those that a mesh axis runs over, the one named last changes fastest.
Arguments:
- states: float32 [128, 524288], P('band', 'dom'), may hold values from -6 to 6
- previous: float32 [128, 524288], P('band', 'dom'), may hold values from -6 to 6
- potential: float32 [524288], P('dom'), may hold values from -2 to 2
- tile_atom: int32 [8192], P('dom'), may hold values from 0 to 511, as said below
- tile_cells: int32 [8192, 128], P('dom'), may hold values from 0 to 4095
- tile_count: int32 [128], P('dom'), may hold values from 8 to 64, as said below
- projectors: float32 [8192, 8, 128], P('dom'), may hold values from -3 to 3
- coupling: float32 [512, 8, 8], P('dom'), may hold values from -2 to 2
- rotation: float32 [128, 128], replicated, may hold values from -0.5 to 0.5
Outputs:
- rotated: float32 [524288, 128], P(('dom', 'band'))
The draws below stay inside these ranges and needn't reach their ends.
Inputs may be any that keep to these rules, and one draw needn't show every extreme that they name: `tile_atom`: atom a belongs to domain a // 4; the atom of a tile belongs to the tile's own domain or to a domain sharing a face with it. Tiles 0 to tile_count - 1 of a domain are live, the others carry nothing. `tile_cells`: cells of the tile's own domain; a cell may repeat.
All inputs are finite; a program needn't handle non-finite values.
Results may differ from the reference program's by a relative error of at most 0.000071.
Values sent between devices are 32-bit elements; how exact they have to be, the bound alone decides.
A program may use at most 64 MiB of HBM per device.

```python
import jax
import jax.numpy as jnp
from jax import lax

NPROJ = 8
CX = 8
CY = 8
CZ = 64
ATOM_DEV = 4
TILES = 64
TILE_PTS = 128
DOMAINS = 128
DGZ = 4
DGY = 4
DGX = 8
CELLS = 4096
NX = 64
NY = 32
NZ = 256
NSTATE = 128
ATOMS = 512
N_DOM = 128


def draw_tile_count(key, part):
    key = jax.random.fold_in(key, 11)
    first_key, second_key = jax.random.split(key)
    levels = jax.random.randint(first_key, (DOMAINS,), 0, 4)
    counts = TILES // jnp.left_shift(jnp.ones((DOMAINS,), jnp.int32), levels)
    chosen = jax.random.randint(second_key, (), 0, DOMAINS)
    return jnp.where(jnp.arange(DOMAINS, dtype=jnp.int32) == chosen, TILES, counts).astype(jnp.int32)


def draw_tile_atom(key, part):
    key = jax.random.fold_in(key, 23)
    first_key, second_key = jax.random.split(key)
    places = jnp.arange(DOMAINS * TILES, dtype=jnp.int32) // TILES
    z_index = places % DGZ
    y_index = places // DGZ % DGY
    x_index = places // (DGZ * DGY)
    heading = jax.random.randint(first_key, (DOMAINS * TILES,), 0, 7)
    x_steps = jnp.array([0, 1, -1, 0, 0, 0, 0], jnp.int32)[heading]
    y_steps = jnp.array([0, 0, 0, 1, -1, 0, 0], jnp.int32)[heading]
    z_steps = jnp.array([0, 0, 0, 0, 0, 1, -1], jnp.int32)[heading]
    x_owner = jnp.clip(x_index + x_steps, 0, DGX - 1)
    y_owner = jnp.clip(y_index + y_steps, 0, DGY - 1)
    z_owner = jnp.clip(z_index + z_steps, 0, DGZ - 1)
    owner = (x_owner * DGY + y_owner) * DGZ + z_owner
    atoms = owner * ATOM_DEV + jax.random.randint(second_key, (DOMAINS * TILES,), 0, ATOM_DEV)
    atoms = atoms.at[0].set(0).at[DOMAINS * TILES - 1].set(ATOMS - 1)
    return atoms.astype(jnp.int32)


def plant(values, rng, smallest, high):
    longest = values.shape.index(max(values.shape))
    spots = []
    for shift in (0, 1):
        where = [jax.random.randint(jax.random.fold_in(rng, axis), (), 0, length) for axis, length in enumerate(values.shape)]
        where[longest] = (where[longest] + shift) % values.shape[longest]
        spots.append(tuple(where))
    return values.at[spots[0]].set(smallest).at[spots[1]].set(high)


def steps_of(stream_key, extent, cuts, low, top_value):
    def one(dim, shards_of):
        draws = jax.random.uniform(jax.random.fold_in(jax.random.fold_in(stream_key, 6), dim), (shards_of,), jnp.float32, low / len(cuts), top_value / len(cuts))
        return jnp.repeat(jnp.exp(draws), extent[dim] // shards_of).reshape((-1,) + (1,) * (len(extent) - dim - 1))

    loudness = one(*cuts[0])
    for cut in cuts[1:]:
        loudness = loudness * one(*cut)
    return loudness


def bell_draw(own_key, shape, scale, limit, pieces=(), kind=jnp.bfloat16):
    entries = scale * jax.random.normal(own_key, shape, jnp.float32)
    if pieces:
        entries = entries * steps_of(own_key, shape, pieces, -0.22, 0.18)
    return jnp.clip(entries, -limit, limit).astype(kind)


def setup_inputs(seed: int = 0) -> dict:
    seeds = jax.random.split(jax.random.key(seed), 10)
    states = bell_draw(seeds[0], (NSTATE, N_DOM * CELLS), 1.0, 6.0, ((0, 4), (1, 128)), jnp.float32)
    previous = bell_draw(seeds[1], (NSTATE, N_DOM * CELLS), 1.0, 6.0, ((0, 4), (1, 128)), jnp.float32)
    potential = jnp.clip(jax.random.uniform(seeds[2], (N_DOM * CELLS,), jnp.float32, -2.0, 2.0) * steps_of(seeds[2], (N_DOM * CELLS,), ((0, 128),), -0.4, 0.0), -2.0, 2.0)
    tile_atom = draw_tile_atom(jax.random.fold_in(seeds[9], 71), 0)
    tile_cells = plant(jax.random.randint(seeds[4], (N_DOM * TILES, TILE_PTS), 0, CELLS), jax.random.fold_in(seeds[4], 1), 0, CELLS - 1).astype(jnp.int32)
    tile_count = draw_tile_count(jax.random.fold_in(seeds[9], 71), 0)
    projectors = bell_draw(seeds[6], (N_DOM * TILES, NPROJ, TILE_PTS), 0.5, 3.0, ((0, 128),), jnp.float32)
    coupling = bell_draw(seeds[7], (ATOMS, NPROJ, NPROJ), NPROJ ** -0.5, 2.0, ((0, 128),), jnp.float32)
    rotation = bell_draw(seeds[8], (NSTATE, NSTATE), NSTATE ** -0.5, 0.5, (), jnp.float32)
    return {"states": states, "previous": previous, "potential": potential, "tile_atom": tile_atom, "tile_cells": tile_cells, "tile_count": tile_count, "projectors": projectors, "coupling": coupling, "rotation": rotation}


stencil_weights = (-5369.0 / 1800.0, 12.0 / 7.0, -15.0 / 56.0, 10.0 / 189.0, -1.0 / 112.0, 2.0 / 1925.0, -1.0 / 16632.0)


def second_differences(fields):
    radius = len(stencil_weights) - 1
    laplace = (3.0 * stencil_weights[0]) * fields
    for dimension in range(3):
        widths = [(radius, radius) if other == dimension else (0, 0) for other in range(3)]
        padded = jnp.pad(fields, widths)
        length = fields.shape[dimension]
        for offset in range(1, radius + 1):
            higher = lax.slice_in_dim(padded, radius + offset, radius + offset + length, axis=dimension)
            lower_side = lax.slice_in_dim(padded, radius - offset, radius - offset + length, axis=dimension)
            laplace = laplace + stencil_weights[offset] * (higher + lower_side)
    return laplace


def reference(states, previous, potential, tile_atom, tile_cells, tile_count, projectors, coupling, rotation):
    highest = lax.Precision.HIGHEST
    slot_index = jnp.arange(TILES, dtype=jnp.int32)
    alive = (slot_index[None, :] < tile_count[:, None]).reshape(-1).astype(jnp.float32)
    weights = projectors * alive[:, None, None]
    domain_of = jnp.arange(DOMAINS * TILES, dtype=jnp.int32) // TILES
    global_cells = (tile_cells + (domain_of * CELLS)[:, None]).astype(jnp.int32)

    def one_state(values):
        fields = values.reshape(DGX, DGY, DGZ, CX, CY, CZ).transpose(0, 3, 1, 4, 2, 5).reshape(NX, NY, NZ)
        laplace = second_differences(fields)
        kinetic = (-0.5 * laplace).reshape(DGX, CX, DGY, CY, DGZ, CZ).transpose(0, 2, 4, 1, 3, 5).reshape(-1)
        picked = values[global_cells]
        partial_value = jnp.sum(weights * picked[:, None, :], axis=2)
        sums = jax.ops.segment_sum(partial_value, tile_atom, num_segments=ATOMS)
        coefficients = jnp.einsum("aij,aj->ai", coupling, sums, precision=highest)
        spread = jnp.sum(weights * coefficients[tile_atom][:, :, None], axis=1)
        projected = jnp.zeros_like(values).at[global_cells].add(spread)
        return 0.15 * (kinetic + potential * values + projected - 8.0 * values)

    filtered = lax.map(one_state, states) - 0.3 * previous
    return lax.dot_general(filtered, rotation, (((0,), (0,)), ((), ())), precision=highest)
```

```python
import functools

import jax
import jax.numpy as jnp
import numpy as np
from jax import lax
from jax.experimental import pallas as pl
from jax.experimental.pallas import tpu as pltpu
from jax.sharding import PartitionSpec as P

MESH = pl.DeviceIdType.MESH
F32 = jnp.float32
BF16 = jnp.bfloat16

STENCIL = (
    -5369.0 / 1800.0,
    12.0 / 7.0,
    -15.0 / 56.0,
    10.0 / 189.0,
    -1.0 / 112.0,
    2.0 / 1925.0,
    -1.0 / 16632.0,
)
W = tuple(-0.075 * w for w in STENCIL)
QUARTER = 1024
LINE = 512


def split(value):
    high = value.astype(BF16)
    return high, (value - high.astype(F32)).astype(BF16)


def split_constant(matrix):
    high = matrix.astype(jnp.bfloat16)
    low = (matrix - high.astype(np.float64)).astype(jnp.bfloat16)
    return np.asarray(high), np.asarray(low)


def z_matrices():
    lane = np.arange(256)
    gap = np.abs(lane[:, None] - lane[None, :])
    weights = np.array(W + (0.0,) * 256)
    inside = np.where((lane[:, None] // 64 == lane[None, :] // 64) & (gap > 0), weights[np.minimum(gap, 7)], 0.0)
    slot = np.arange(128)
    cell = np.arange(QUARTER)
    same = slot[:, None] // 8 == cell[None, :] // 64
    z = cell[None, :] % 64
    i = slot[:, None] % 8
    used = same & (i < 6)
    pick_high = (used & (z == 58 + i)).astype(np.float64)
    pick_low = (used & (z == i)).astype(np.float64)
    below = np.where(used, weights[np.minimum(z + 6 - i, 7)], 0.0)
    above = np.where(used, weights[np.minimum(64 + i - z, 7)], 0.0)
    pick = np.concatenate([pick_high, pick_low]).astype(jnp.bfloat16)
    return *split_constant(inside), pick, *split_constant(np.concatenate([below, above]))


def dot(a, b, ca=1, cb=0):
    return lax.dot_general(a, b, (((ca,), (cb,)), ((), ())), preferred_element_type=F32)


def kernel(
    count_ref,
    states,
    previous,
    potential,
    tile_atom,
    tile_cells,
    projectors,
    coupling,
    rotation,
    in_hi,
    in_lo,
    pick,
    face_hi,
    face_lo,
    out,
    filt,
    y_land,
    x_send,
    x_land,
    z_send,
    z_land,
    s_send,
    s_land,
    c_send,
    c_land,
    f_land,
    g_hi,
    g_lo,
    member,
    y_ss,
    y_rs,
    x_ss,
    x_rs,
    z_ss,
    z_rs,
    s_ss,
    s_rs,
    c_ss,
    c_rs,
    f_ss,
    f_rs,
):
    band = lax.axis_index("band")
    dom = lax.axis_index("dom")
    gz = lax.rem(dom, 4)
    gy = lax.rem(dom // 4, 4)
    gx = dom // 16
    steps = (16, -16, 4, -4, 1, -1)
    exists = (gx < 7, gx > 0, gy < 3, gy > 0, gz < 3, gz > 0)

    def there(direction):
        return (band, dom + steps[direction])

    def lanes(quarter):
        return pl.multiple_of(quarter * QUARTER, QUARTER)

    barrier = pltpu.get_barrier_semaphore()
    for direction in range(6):

        @pl.when(exists[direction])
        def _():
            pl.semaphore_signal(barrier, inc=1, device_id=there(direction), device_id_type=MESH)

    for other in range(1, 4):
        pl.semaphore_signal(
            barrier, inc=1, device_id=(lax.rem(band + other, 4), dom), device_id_type=MESH
        )
    partners = 3
    for direction in range(6):
        partners = partners + jnp.where(exists[direction], 1, 0)
    pl.semaphore_wait(barrier, partners)

    def y_copies(side, k):
        quarter = lax.rem(band + 1 + k, 4)
        copies = []
        for i in range(2):
            start = pl.multiple_of(lanes(quarter) + i * LINE + (128 if side == 0 else 0), 128)
            copies.append(
                pltpu.make_async_remote_copy(
                    src_ref=states.at[:, pl.ds(start, 384)],
                    dst_ref=y_land.at[side, :, pl.ds(start, 384)],
                    send_sem=y_ss.at[side, k, i],
                    recv_sem=y_rs.at[side, k, i],
                    device_id=there(2 + side),
                    device_id_type=MESH,
                )
            )
        return copies

    def y_start(k, _):
        for side in range(2):

            @pl.when(exists[2 + side])
            def _():
                for copy in y_copies(side, k):
                    copy.start()

        return 0

    lax.fori_loop(0, 4, y_start, 0)

    def x_parts(g, _):
        rows = pl.ds(pl.multiple_of(g * 8, 8), 8)
        for column in range(4):
            layer = [states[rows, pl.ds(x * LINE + column * 128, 128)] for x in range(8)]
            for target in range(6):
                total = W[6] * layer[target + 2]
                for m in range(target + 3, 8):
                    total = total + W[target + 8 - m] * layer[m]
                x_send[0, rows, pl.ds(target * LINE + column * 128, 128)] = total
            for target in range(2, 8):
                total = W[6] * layer[target - 2]
                for m in range(target - 2):
                    total = total + W[m + 8 - target] * layer[m]
                x_send[1, rows, pl.ds(target * LINE + column * 128, 128)] = total
        return 0

    lax.fori_loop(0, 4, x_parts, 0)

    def x_copy(side, k):
        quarter = lax.rem(band + 1 + k, 4)
        block = pl.ds(lanes(quarter), QUARTER)
        return pltpu.make_async_remote_copy(
            src_ref=x_send.at[side, :, block],
            dst_ref=x_land.at[side, :, block],
            send_sem=x_ss.at[side, k],
            recv_sem=x_rs.at[side, k],
            device_id=there(side),
            device_id_type=MESH,
        )

    def x_used(side, k):
        quarter = lax.rem(band + 1 + k, 4)
        return quarter < 3 if side == 0 else quarter > 0

    def x_start(k, _):
        for side in range(2):

            @pl.when(exists[side] & x_used(side, k))
            def _():
                x_copy(side, k).start()

        return 0

    lax.fori_loop(0, 4, x_start, 0)

    pieces = []
    for quarter in range(4):
        pieces.extend(split(states[:, pl.ds(quarter * QUARTER, QUARTER)]))
    picked = dot(jnp.concatenate(pieces, axis=0), pick[...], 1, 1)
    for quarter in range(4):
        both = picked[quarter * 64 : quarter * 64 + 32] + picked[quarter * 64 + 32 : quarter * 64 + 64]
        z_send[0, :, pl.ds(quarter * 128, 128)] = both[:, 0:128]
        z_send[1, :, pl.ds(quarter * 128, 128)] = both[:, 128:256]

    def z_copy(side):
        return pltpu.make_async_remote_copy(
            src_ref=z_send.at[side],
            dst_ref=z_land.at[side],
            send_sem=z_ss.at[side],
            recv_sem=z_rs.at[side],
            device_id=there(4 + side),
            device_id_type=MESH,
        )

    for side in range(2):

        @pl.when(exists[4 + side])
        def _():
            z_copy(side).start()

        @pl.when(jnp.logical_not(exists[5 - side]))
        def _():
            z_land[side] = jnp.zeros((32, 512), F32)

        @pl.when(jnp.logical_not(exists[3 - side]))
        def _():
            y_land[side] = jnp.zeros((32, 4096), F32)

    def tile_pair(pair, _):
        spread = []
        for which in range(2):
            t = pair * 2 + which
            cells = tile_cells[pl.ds(t, 1), :]
            high, low = cells >> 8, cells & 255
            w = projectors[t]
            w_hi = w.astype(BF16).astype(F32)
            w_lo = w - w_hi
            blocks_hi, blocks_lo = [], []
            for h in range(16):
                here = high == h
                blocks_hi.append(jnp.where(here, w_hi, 0.0))
                blocks_lo.append(jnp.where(here, w_lo, 0.0))
            left = jnp.concatenate(
                [jnp.concatenate(blocks_hi, 0).astype(BF16), jnp.concatenate(blocks_lo, 0).astype(BF16)], axis=1
            )
            hot = jnp.where(lax.broadcasted_iota(jnp.int32, (256, 128), 0) == low, 1.0, 0.0).astype(BF16)
            spread.append(dot(left, jnp.concatenate([hot, hot], axis=1), 1, 1))
        rows = pl.ds(pl.multiple_of(pair * 16, 16), 16)
        for h in range(16):
            both = jnp.concatenate([spread[0][h * 8 : h * 8 + 8], spread[1][h * 8 : h * 8 + 8]], axis=0)
            both_hi, both_lo = split(both)
            g_hi[rows, pl.ds(h * 256, 256)] = both_hi
            g_lo[rows, pl.ds(h * 256, 256)] = both_lo
        return 0

    lax.fori_loop(0, 32, tile_pair, 0)

    relative = (tile_atom[...] - dom * 4).astype(F32).astype(BF16)
    repeat = (
        lax.broadcasted_iota(jnp.int32, (64, 512), 0) == lax.broadcasted_iota(jnp.int32, (64, 512), 1) // 8
    )
    owner = dot(
        jnp.broadcast_to(relative.astype(F32), (16, 64)).astype(BF16), jnp.where(repeat, 1.0, 0.0).astype(BF16)
    )[0:1]
    slot = lax.broadcasted_iota(jnp.int32, (1, 512), 1)
    owner = jnp.where(slot // 8 < count_ref[0], owner, 1000.0)
    row = lax.broadcasted_iota(jnp.int32, (32, 512), 0)
    same_j = (row & 7) == (lax.broadcasted_iota(jnp.int32, (32, 512), 1) & 7)
    atom = (row // 8).astype(F32)
    for number, step in enumerate((0,) + steps):
        match = same_j & (atom + 4.0 * step == owner)
        member[pl.ds(number * 32, 32), :] = jnp.where(match, 1.0, 0.0).astype(BF16)

    st_hi, st_lo = split(states[...])
    partial_hi = dot(g_hi[...], jnp.concatenate([st_hi, st_lo], axis=0), 1, 1)
    partial_value = partial_hi[:, 0:32] + partial_hi[:, 32:64] + dot(g_lo[...], st_hi, 1, 1)
    part_hi, part_lo = split(partial_value)
    sums = dot(member[...], part_hi) + dot(member[...], part_lo)
    messages = []
    for number in range(7):
        messages.append(
            jnp.concatenate([sums[number * 32 + a * 8 : number * 32 + a * 8 + 8] for a in range(4)], axis=1)
        )
    for direction in range(6):
        s_send[direction] = messages[direction + 1]

    def s_copy(direction):
        return pltpu.make_async_remote_copy(
            src_ref=s_send.at[direction],
            dst_ref=s_land.at[direction],
            send_sem=s_ss.at[direction],
            recv_sem=s_rs.at[direction],
            device_id=there(direction),
            device_id_type=MESH,
        )

    for direction in range(6):

        @pl.when(exists[direction])
        def _():
            s_copy(direction).start()

        @pl.when(jnp.logical_not(exists[direction ^ 1]))
        def _():
            s_land[direction] = jnp.zeros((8, 128), F32)
            c_land[direction] = jnp.zeros((8, 128), F32)

    def base(g, _):
        rows = pl.ds(pl.multiple_of(g * 8, 8), 8)
        for column in range(4):
            layer = [states[rows, pl.ds(x * LINE + column * 128, 128)] for x in range(8)]
            for x in range(8):
                block = pl.ds(x * LINE + column * 128, 128)
                total = layer[x] * (3.0 * W[0] - 1.2 + 0.15 * potential[:, block]) - 0.3 * previous[rows, block]
                for k in range(1, 7):
                    pair = [layer[m] for m in (x - k, x + k) if 0 <= m < 8]
                    if pair:
                        total = total + W[k] * (pair[0] + pair[1] if len(pair) == 2 else pair[0])
                filt[rows, block] = total
        return 0

    lax.fori_loop(0, 4, base, 0)
    blocks = [states[:, pl.ds(i * 256, 256)] for i in range(16)]
    tall_hi, tall_lo = split(jnp.concatenate(blocks, axis=0))
    inside = dot(tall_hi, in_hi[...]) + dot(tall_lo, in_hi[...]) + dot(tall_hi, in_lo[...])
    for i in range(16):
        filt[:, pl.ds(i * 256, 256)] += inside[i * 32 : i * 32 + 32]

    for side in range(2):

        @pl.when(exists[5 - side])
        def _():
            z_copy(side).wait_recv()

    faces = []
    for quarter in range(4):
        block = pl.ds(quarter * 128, 128)
        faces.append(jnp.concatenate([z_land[0, :, block], z_land[1, :, block]], axis=1))
    faces_hi, faces_lo = split(jnp.concatenate(faces, axis=0))
    edge = dot(faces_hi, face_hi[...]) + dot(faces_lo, face_hi[...]) + dot(faces_hi, face_lo[...])
    for quarter in range(4):
        filt[:, pl.ds(quarter * QUARTER, QUARTER)] += edge[quarter * 32 : quarter * 32 + 32]

    owned = messages[0]
    for direction in range(6):

        @pl.when(exists[direction ^ 1])
        def _():
            s_copy(direction).wait_recv()

        owned = owned + s_land[direction]
    lane = lax.broadcasted_iota(jnp.int32, (8, 128), 1) // 32
    coef = jnp.zeros((8, 128), F32)
    for j in range(8):
        column = jnp.zeros((8, 128), F32)
        for a in range(4):
            column = jnp.where(lane == a, coupling[a][:, j : j + 1], column)
        coef = coef + column * owned[j : j + 1, :]
    c_send[...] = coef

    def c_copy(direction):
        return pltpu.make_async_remote_copy(
            src_ref=c_send,
            dst_ref=c_land.at[direction],
            send_sem=c_ss.at[direction],
            recv_sem=c_rs.at[direction],
            device_id=there(direction),
            device_id_type=MESH,
        )

    for direction in range(6):

        @pl.when(exists[direction])
        def _():
            c_copy(direction).start()

    for direction in range(6):

        @pl.when(exists[direction ^ 1])
        def _():
            c_copy(direction).wait_recv()

    known = [coef] + [c_land[direction ^ 1] for direction in range(6)]
    table = jnp.concatenate([block[:, a * 32 : a * 32 + 32] for block in known for a in range(4)], axis=0)
    table_hi, table_lo = split(table)
    tile_coef = dot(jnp.concatenate([table_hi, table_lo], axis=1).T, member[...]).astype(BF16)

    def project(i, _):
        block = pl.ds(pl.multiple_of(i * 512, 512), 512)
        both = dot(tile_coef, g_hi[:, block])
        more = dot(tile_coef[0:32], g_lo[:, block])
        filt[:, block] += 0.15 * (both[0:32] + both[32:64] + more)
        return 0

    lax.fori_loop(0, 8, project, 0)

    left_half = lax.broadcasted_iota(jnp.int32, (8, 128), 1) < 64

    def finish(quarter):
        def line(n, _):
            rows = pl.ds(pl.multiple_of(lax.rem(n, 4) * 8, 8), 8)
            start = lanes(quarter) + n // 4 * LINE

            def at(offset):
                return pl.ds(pl.multiple_of(start + offset, 128), 128)

            run = [y_land[0, rows, at(128 + 128 * i)] for i in range(3)]
            run += [states[rows, at(128 * i)] for i in range(4)]
            run += [y_land[1, rows, at(128 * i)] for i in range(3)]
            turned = [pltpu.roll(v, 64, 1) for v in run]
            odd = []
            for g in range(3, 8):
                odd.append(
                    W[1] * (turned[g] + turned[g - 1])
                    + W[3] * (turned[min(g + 1, 9)] + turned[g - 2])
                    + W[5] * (turned[min(g + 2, 9)] + turned[g - 3])
                )
            for g in range(4):
                total = filt[rows, at(128 * g)]
                for k in (2, 4, 6):
                    total = total + W[k] * (run[g + 3 + k // 2] + run[g + 3 - k // 2])
                filt[rows, at(128 * g)] = total + jnp.where(left_half, odd[g], odd[g + 1])
            return 0

        lax.fori_loop(0, 8, line, 0)

    def f_copy(k):
        quarter = lax.rem(band + 1 + k, 4)
        return pltpu.make_async_remote_copy(
            src_ref=filt.at[:, pl.ds(lanes(quarter), QUARTER)],
            dst_ref=f_land.at[k],
            send_sem=f_ss.at[k],
            recv_sem=f_rs.at[k],
            device_id=(quarter, dom),
            device_id_type=MESH,
        )

    def rotate(value, source, first):
        v_hi, v_lo = split(value)
        r_hi, r_lo = split(rotation[pl.ds(pl.multiple_of(source * 32, 32), 32), :])
        product = dot(
            jnp.concatenate([v_hi, v_lo, v_hi], axis=0), jnp.concatenate([r_hi, r_hi, r_lo], axis=0), 0, 0
        )
        if first:
            out[...] = product
        else:
            out[...] += product

    def arrived(k, first):
        f_copy(k).wait_recv()
        rotate(f_land[k], lax.rem(band + 3 - k, 4), first)

    for k in range(4):
        quarter = lax.rem(band + 1 + k, 4)
        for side in range(2):

            @pl.when(exists[side ^ 1] & x_used(side, k))
            def _():
                x_copy(side, k).wait_recv()
                block = pl.ds(lanes(quarter), QUARTER)
                filt[:, block] += x_land[side, :, block]

            @pl.when(exists[3 - side])
            def _():
                for copy in y_copies(side, k):
                    copy.wait_recv()

        finish(quarter)
        if k < 3:
            f_copy(k).start()
        if k > 0:
            arrived(k - 1, k == 1)
    rotate(filt[:, pl.ds(lanes(band), QUARTER)], band, False)

    for k in range(4):
        for side in range(2):

            @pl.when(exists[side] & x_used(side, k))
            def _():
                x_copy(side, k).wait_send()

            @pl.when(exists[2 + side])
            def _():
                for copy in y_copies(side, k):
                    copy.wait_send()

    for side in range(2):

        @pl.when(exists[4 + side])
        def _():
            z_copy(side).wait_send()

    for direction in range(6):

        @pl.when(exists[direction])
        def _():
            s_copy(direction).wait_send()
            c_copy(direction).wait_send()

    for k in range(3):
        f_copy(k).wait_send()


def body(states, previous, potential, tile_atom, tile_cells, tile_count, projectors, coupling, rotation):
    vmem = pl.BlockSpec(memory_space=pltpu.VMEM)
    dma = pltpu.SemaphoreType.DMA
    return pl.pallas_call(
        kernel,
        out_shape=jax.ShapeDtypeStruct((QUARTER, 128), F32),
        in_specs=[pl.BlockSpec(memory_space=pltpu.SMEM)] + [vmem] * 13,
        out_specs=vmem,
        scratch_shapes=[
            pltpu.VMEM((32, 4096), F32),
            pltpu.VMEM((2, 32, 4096), F32),
            pltpu.VMEM((2, 32, 4096), F32),
            pltpu.VMEM((2, 32, 4096), F32),
            pltpu.VMEM((2, 32, 512), F32),
            pltpu.VMEM((2, 32, 512), F32),
            pltpu.VMEM((6, 8, 128), F32),
            pltpu.VMEM((6, 8, 128), F32),
            pltpu.VMEM((8, 128), F32),
            pltpu.VMEM((6, 8, 128), F32),
            pltpu.VMEM((3, 32, QUARTER), F32),
            pltpu.VMEM((512, 4096), BF16),
            pltpu.VMEM((512, 4096), BF16),
            pltpu.VMEM((224, 512), BF16),
            dma((2, 4, 2)),
            dma((2, 4, 2)),
            dma((2, 4)),
            dma((2, 4)),
            dma((2,)),
            dma((2,)),
            dma((6,)),
            dma((6,)),
            dma((6,)),
            dma((6,)),
            dma((3,)),
            dma((3,)),
        ],
        compiler_params=pltpu.CompilerParams(
            collective_id=0, has_side_effects=True, vmem_limit_bytes=48 * 1024 * 1024
        ),
        name="chebyshev_step",
    )(
        tile_count,
        states,
        previous,
        potential.reshape(1, -1),
        tile_atom.reshape(1, -1),
        tile_cells,
        projectors,
        coupling,
        rotation,
        *(jnp.asarray(m) for m in z_matrices()),
    )


def solution(mesh):
    placed = (
        P("band", "dom"),
        P("band", "dom"),
        P("dom"),
        P("dom"),
        P("dom", None),
        P("dom"),
        P("dom", None, None),
        P("dom", None, None),
        P(),
    )
    return jax.shard_map(
        body, mesh=mesh, in_specs=placed, out_specs=P(("dom", "band"), None), check_vma=False
    )
```

```python
import jax
import jax.numpy as jnp
from jax import lax
from jax.experimental import pallas as pl
from jax.experimental.pallas import tpu as pltpu
from jax.sharding import PartitionSpec as P

MESH = pl.DeviceIdType.MESH
F32 = jnp.float32
BF16 = jnp.bfloat16

STENCIL = (
    -5369.0 / 1800.0,
    12.0 / 7.0,
    -15.0 / 56.0,
    10.0 / 189.0,
    -1.0 / 112.0,
    2.0 / 1925.0,
    -1.0 / 16632.0,
)
W = tuple(-0.075 * w for w in STENCIL)
QUARTER = 1024
LINE = 512


def split(value):
    high = value.astype(BF16)
    return high, (value - high.astype(F32)).astype(BF16)


def faces_of(rows, columns):
    row = lax.broadcasted_iota(jnp.int32, (rows, 1), 0)
    column = lax.broadcasted_iota(jnp.int32, (rows, columns), 1)
    side, line, i = row // 128, (row // 8 & 15) * 64, row & 7
    used = i < 6
    cell = jnp.where(used, line + jnp.where(side == 0, 58 + i, i), -1)
    pick = jnp.where(column == cell, 1.0, 0.0).astype(BF16)
    face = jnp.zeros((rows, columns), F32)
    for n in range(1, 7):
        z = jnp.where(side == 0, n - 6 + i, 64 + i - n)
        place = jnp.where(used & (z >= 0) & (z < 64), line + z, -1)
        face = jnp.where(column == place, W[n], face)
    return pick, *split(face)


def inside_of(size):
    row = lax.broadcasted_iota(jnp.int32, (size, size), 0)
    column = lax.broadcasted_iota(jnp.int32, (size, size), 1)
    gap = jnp.where(row // 64 == column // 64, jnp.abs(row - column), 0)
    weight = jnp.zeros((size, size), F32)
    for n in range(1, 7):
        weight = jnp.where(gap == n, W[n], weight)
    return split(weight)


def dot(a, b, ca=1, cb=0):
    return lax.dot_general(a, b, (((ca,), (cb,)), ((), ())), preferred_element_type=F32)


def kernel(
    count_ref,
    states_in,
    previous_in,
    potential_in,
    atom_in,
    cells_in,
    projectors_in,
    coupling_in,
    rotation_in,
    out,
    states,
    previous,
    potential,
    tile_atom,
    tile_cells,
    projectors,
    coupling,
    rotation,
    load_sem,
    face_hi,
    face_lo,
    filt,
    y_land,
    x_send,
    x_land,
    z_send,
    z_land,
    s_send,
    s_land,
    c_send,
    c_land,
    f_land,
    g_hi,
    g_lo,
    member,
    y_ss,
    y_rs,
    x_ss,
    x_rs,
    z_ss,
    z_rs,
    s_ss,
    s_rs,
    c_ss,
    c_rs,
    f_ss,
    f_rs,
):
    band = lax.axis_index("band")
    dom = lax.axis_index("dom")
    gz = lax.rem(dom, 4)
    gy = lax.rem(dom // 4, 4)
    gx = dom // 16
    steps = (16, -16, 4, -4, 1, -1)
    exists = (gx < 7, gx > 0, gy < 3, gy > 0, gz < 3, gz > 0)

    loads = [
        pltpu.make_async_copy(source, target, load_sem.at[n])
        for n, (source, target) in enumerate(
            (
                (states_in, states),
                (cells_in, tile_cells),
                (projectors_in, projectors),
                (atom_in, tile_atom),
                (previous_in, previous),
                (potential_in, potential),
                (coupling_in, coupling),
                (rotation_in, rotation),
            )
        )
    ]
    for load in loads:
        load.start()

    def there(direction):
        return (band, dom + steps[direction])

    def quarter_of(k):
        return lax.rem(band + 1 + k, 4)

    def lanes(quarter):
        return pl.multiple_of(quarter * QUARTER, QUARTER)

    def remote(source, target, sent, landed, device):
        return pltpu.make_async_remote_copy(
            src_ref=source,
            dst_ref=target,
            send_sem=sent,
            recv_sem=landed,
            device_id=device,
            device_id_type=MESH,
        )

    def start(needed, copies):
        @pl.when(needed)
        def _():
            for copy in copies():
                copy.start()

    def landed(needed, copies):
        @pl.when(needed)
        def _():
            for copy in copies():
                copy.wait_recv()

    def sent(needed, copies):
        @pl.when(needed)
        def _():
            for copy in copies():
                copy.wait_send()

    outer = (gy == 0) | (gy == 3)
    inner = jnp.logical_not(outer)
    even = lax.rem(gy, 2) == 0
    partner = (band, jnp.where(even, dom + 4, dom - 4))
    far = (band, jnp.where(gy < 2, dom + 8, dom - 8))
    partner_side = jnp.where(even, 1, 0)
    six = jnp.where(gy == 0, 128, 0)

    barrier = pltpu.get_barrier_semaphore()
    for direction in range(6):

        @pl.when(exists[direction])
        def _():
            pl.semaphore_signal(barrier, inc=1, device_id=there(direction), device_id_type=MESH)

    for other in range(1, 4):
        pl.semaphore_signal(
            barrier, inc=1, device_id=(lax.rem(band + other, 4), dom), device_id_type=MESH
        )
    pl.semaphore_signal(barrier, inc=1, device_id=far, device_id_type=MESH)
    partners = 4
    for direction in range(6):
        partners = partners + jnp.where(exists[direction], 1, 0)
    pl.semaphore_wait(barrier, partners)

    def y_all(k):
        block = pl.ds(lanes(quarter_of(k)), QUARTER)
        return [
            remote(states_in.at[:, block], y_land.at[1 - partner_side, :, block], y_ss.at[0, k], y_rs.at[0, k], partner)
        ]

    def y_six(source, number, k, device):
        copies = []
        for i in range(2):
            block = pl.ds(pl.multiple_of(lanes(quarter_of(k)) + i * LINE + six, 128), 384)
            copies.append(
                remote(
                    source.at[:, block],
                    y_land.at[1 - partner_side, :, block],
                    y_ss.at[number + i, k],
                    y_rs.at[number + i, k],
                    device,
                )
            )
        return copies

    def y_outer(k):
        return y_six(states_in, 1, k, partner)

    def y_relay(k):
        return y_six(y_land.at[partner_side], 3, k, far)

    def y_start(k):
        start(inner, lambda: y_all(k))
        start(outer, lambda: y_outer(k))

    def hand_on(k):
        landed(outer, lambda: y_all(k))
        start(outer, lambda: y_relay(k))

    def x_copy(side, k):
        block = pl.ds(lanes(quarter_of(k)), QUARTER)
        return [
            remote(
                x_send.at[side, :, block], x_land.at[side, :, block], x_ss.at[side, k], x_rs.at[side, k], there(side)
            )
        ]

    def x_used(side, k):
        return quarter_of(k) < 3 if side == 0 else quarter_of(k) > 0

    def x_start(k):
        for side in range(2):
            start(exists[side] & x_used(side, k), lambda: x_copy(side, k))

    def z_copy(side):
        return [remote(z_send.at[side], z_land.at[side], z_ss.at[side], z_rs.at[side], there(4 + side))]

    def s_copy(direction):
        return [
            remote(
                s_send.at[direction], s_land.at[direction], s_ss.at[direction], s_rs.at[direction], there(direction)
            )
        ]

    def c_copy(direction):
        return [remote(c_send, c_land.at[direction], c_ss.at[direction], c_rs.at[direction], there(direction))]

    def f_copy(k):
        return [
            remote(
                filt.at[:, pl.ds(lanes(quarter_of(k)), QUARTER)],
                f_land.at[k],
                f_ss.at[k],
                f_rs.at[k],
                (quarter_of(k), dom),
            )
        ]

    y_start(0)

    def x_parts(g, _):
        rows = pl.ds(pl.multiple_of(g * 8, 8), 8)
        for column in range(4):
            layer = [states[rows, pl.ds(x * LINE + column * 128, 128)] for x in range(8)]
            for target in range(6):
                total = W[6] * layer[target + 2]
                for m in range(target + 3, 8):
                    total = total + W[target + 8 - m] * layer[m]
                x_send[0, rows, pl.ds(target * LINE + column * 128, 128)] = total
            for target in range(2, 8):
                total = W[6] * layer[target - 2]
                for m in range(target - 2):
                    total = total + W[m + 8 - target] * layer[m]
                x_send[1, rows, pl.ds(target * LINE + column * 128, 128)] = total
        return 0

    loads[0].wait()
    lax.fori_loop(0, 4, x_parts, 0)
    x_start(0)

    pick, *face = faces_of(256, QUARTER)
    face_hi[...], face_lo[...] = face
    pieces = []
    for quarter in range(4):
        pieces.extend(split(states[:, pl.ds(quarter * QUARTER, QUARTER)]))
    picked = dot(jnp.concatenate(pieces, axis=0), pick, 1, 1)
    for quarter in range(4):
        both = picked[quarter * 64 : quarter * 64 + 32] + picked[quarter * 64 + 32 : quarter * 64 + 64]
        z_send[0, :, pl.ds(quarter * 128, 128)] = both[:, 0:128]
        z_send[1, :, pl.ds(quarter * 128, 128)] = both[:, 128:256]

    for side in range(2):
        start(exists[4 + side], lambda: z_copy(side))

        @pl.when(jnp.logical_not(exists[5 - side]))
        def _():
            z_land[side] = jnp.zeros((32, 512), F32)

        @pl.when(jnp.logical_not(exists[3 - side]))
        def _():
            y_land[side] = jnp.zeros((32, 4096), F32)

    for direction in range(6):

        @pl.when(jnp.logical_not(exists[direction ^ 1]))
        def _():
            s_land[direction] = jnp.zeros((8, 128), F32)
            c_land[direction] = jnp.zeros((8, 128), F32)

    loads[1].wait()
    loads[2].wait()

    def tile_pair(pair, _):
        spread = []
        for which in range(2):
            t = pair * 2 + which
            cells = tile_cells[pl.ds(t, 1), :]
            high, low = cells >> 8, cells & 255
            w = projectors[t]
            w_hi = w.astype(BF16).astype(F32)
            w_lo = w - w_hi
            blocks_hi, blocks_lo = [], []
            for h in range(16):
                here = high == h
                blocks_hi.append(jnp.where(here, w_hi, 0.0))
                blocks_lo.append(jnp.where(here, w_lo, 0.0))
            left = jnp.concatenate(
                [jnp.concatenate(blocks_hi, 0).astype(BF16), jnp.concatenate(blocks_lo, 0).astype(BF16)], axis=1
            )
            hot = jnp.where(lax.broadcasted_iota(jnp.int32, (256, 128), 0) == low, 1.0, 0.0).astype(BF16)
            spread.append(dot(left, jnp.concatenate([hot, hot], axis=1), 1, 1))
        rows = pl.ds(pl.multiple_of(pair * 16, 16), 16)
        for h in range(16):
            both = jnp.concatenate([spread[0][h * 8 : h * 8 + 8], spread[1][h * 8 : h * 8 + 8]], axis=0)
            both_hi, both_lo = split(both)
            g_hi[rows, pl.ds(h * 256, 256)] = both_hi
            g_lo[rows, pl.ds(h * 256, 256)] = both_lo
        return 0

    lax.fori_loop(0, 32, tile_pair, 0)

    loads[3].wait()
    relative = (tile_atom[...] - dom * 4).astype(F32).astype(BF16)
    repeat = (
        lax.broadcasted_iota(jnp.int32, (64, 512), 0) == lax.broadcasted_iota(jnp.int32, (64, 512), 1) // 8
    )
    owner = dot(
        jnp.broadcast_to(relative.astype(F32), (16, 64)).astype(BF16), jnp.where(repeat, 1.0, 0.0).astype(BF16)
    )[0:1]
    slot = lax.broadcasted_iota(jnp.int32, (1, 512), 1)
    owner = jnp.where(slot // 8 < count_ref[0], owner, 1000.0)
    row = lax.broadcasted_iota(jnp.int32, (32, 512), 0)
    same_j = (row & 7) == (lax.broadcasted_iota(jnp.int32, (32, 512), 1) & 7)
    atom = (row // 8).astype(F32)
    for number, step in enumerate((0,) + steps):
        match = same_j & (atom + 4.0 * step == owner)
        member[pl.ds(number * 32, 32), :] = jnp.where(match, 1.0, 0.0).astype(BF16)

    st_hi, st_lo = split(states[...])
    partial_hi = dot(g_hi[...], jnp.concatenate([st_hi, st_lo], axis=0), 1, 1)
    partial_value = partial_hi[:, 0:32] + partial_hi[:, 32:64] + dot(g_lo[...], st_hi, 1, 1)
    part_hi, part_lo = split(partial_value)
    sums = dot(member[...], part_hi) + dot(member[...], part_lo)
    messages = []
    for number in range(7):
        messages.append(
            jnp.concatenate([sums[number * 32 + a * 8 : number * 32 + a * 8 + 8] for a in range(4)], axis=1)
        )
    for direction in range(6):
        s_send[direction] = messages[direction + 1]
    for direction in range(6):
        start(exists[direction], lambda: s_copy(direction))
    y_start(1)
    x_start(1)

    def base(g, _):
        rows = pl.ds(pl.multiple_of(g * 8, 8), 8)
        for column in range(4):
            layer = [states[rows, pl.ds(x * LINE + column * 128, 128)] for x in range(8)]
            for x in range(8):
                block = pl.ds(x * LINE + column * 128, 128)
                total = layer[x] * (3.0 * W[0] - 1.2 + 0.15 * potential[:, block]) - 0.3 * previous[rows, block]
                for k in range(1, 7):
                    pair = [layer[m] for m in (x - k, x + k) if 0 <= m < 8]
                    if pair:
                        total = total + W[k] * (pair[0] + pair[1] if len(pair) == 2 else pair[0])
                filt[rows, block] = total
        return 0

    for n in (4, 5):
        loads[n].wait()
    lax.fori_loop(0, 4, base, 0)
    blocks = [states[:, pl.ds(i * 256, 256)] for i in range(16)]
    tall_hi, tall_lo = split(jnp.concatenate(blocks, axis=0))
    in_hi, in_lo = inside_of(256)
    inside = dot(tall_hi, in_hi) + dot(tall_lo, in_hi) + dot(tall_hi, in_lo)
    for i in range(16):
        filt[:, pl.ds(i * 256, 256)] += inside[i * 32 : i * 32 + 32]

    hand_on(0)

    for side in range(2):
        landed(exists[5 - side], lambda: z_copy(side))
    faces = []
    for quarter in range(4):
        block = pl.ds(quarter * 128, 128)
        faces.append(jnp.concatenate([z_land[0, :, block], z_land[1, :, block]], axis=1))
    faces_hi, faces_lo = split(jnp.concatenate(faces, axis=0))
    edge = dot(faces_hi, face_hi[...]) + dot(faces_lo, face_hi[...]) + dot(faces_hi, face_lo[...])
    for quarter in range(4):
        filt[:, pl.ds(quarter * QUARTER, QUARTER)] += edge[quarter * 32 : quarter * 32 + 32]

    loads[6].wait()
    loads[7].wait()
    lane = lax.broadcasted_iota(jnp.int32, (8, 128), 1) // 32
    mixing = []
    for j in range(8):
        column = jnp.zeros((8, 128), F32)
        for a in range(4):
            column = jnp.where(lane == a, coupling[a][:, j : j + 1], column)
        mixing.append(column)
    owned = messages[0]
    for direction in range(6):
        landed(exists[direction ^ 1], lambda: s_copy(direction))
        owned = owned + s_land[direction]
    coef = mixing[0] * owned[0:1, :]
    for j in range(1, 8):
        coef = coef + mixing[j] * owned[j : j + 1, :]
    c_send[...] = coef
    for direction in range(6):
        start(exists[direction], lambda: c_copy(direction))
    for k in (2, 3):
        y_start(k)
        x_start(k)

    hand_on(1)

    for direction in range(6):
        landed(exists[direction ^ 1], lambda: c_copy(direction))
    known = [coef] + [c_land[direction ^ 1] for direction in range(6)]
    table = jnp.concatenate([block[:, a * 32 : a * 32 + 32] for block in known for a in range(4)], axis=0)
    table_hi, table_lo = split(table)
    tile_coef = dot(jnp.concatenate([table_hi, table_lo], axis=1).T, member[...]).astype(BF16)

    def project(i, _):
        block = pl.ds(pl.multiple_of(i * 512, 512), 512)
        both = dot(tile_coef, g_hi[:, block])
        more = dot(tile_coef[0:32], g_lo[:, block])
        filt[:, block] += 0.15 * (both[0:32] + both[32:64] + more)
        return 0

    lax.fori_loop(0, 8, project, 0)

    left_half = lax.broadcasted_iota(jnp.int32, (8, 128), 1) < 64

    def finish(k):
        quarter = quarter_of(k)
        for side in range(2):

            @pl.when(exists[side ^ 1] & x_used(side, k))
            def _():
                x_copy(side, k)[0].wait_recv()
                block = pl.ds(lanes(quarter), QUARTER)
                filt[:, block] += x_land[side, :, block]

        landed(inner, lambda: y_outer(k))
        landed(inner, lambda: y_relay(k))

        def line(n, _):
            rows = pl.ds(pl.multiple_of(lax.rem(n, 4) * 8, 8), 8)
            begin = lanes(quarter) + n // 4 * LINE

            def at(offset):
                return pl.ds(pl.multiple_of(begin + offset, 128), 128)

            run = [y_land[0, rows, at(128 + 128 * i)] for i in range(3)]
            run += [states[rows, at(128 * i)] for i in range(4)]
            run += [y_land[1, rows, at(128 * i)] for i in range(3)]
            turned = [pltpu.roll(v, 64, 1) for v in run]
            odd = []
            for g in range(3, 8):
                odd.append(
                    W[1] * (turned[g] + turned[g - 1])
                    + W[3] * (turned[min(g + 1, 9)] + turned[g - 2])
                    + W[5] * (turned[min(g + 2, 9)] + turned[g - 3])
                )
            for g in range(4):
                total = filt[rows, at(128 * g)]
                for n_far in (2, 4, 6):
                    total = total + W[n_far] * (run[g + 3 + n_far // 2] + run[g + 3 - n_far // 2])
                filt[rows, at(128 * g)] = total + jnp.where(left_half, odd[g], odd[g + 1])
            return 0

        lax.fori_loop(0, 8, line, 0)

    def rotate(value, source, first):
        v_hi, v_lo = split(value)
        r_hi, r_lo = split(rotation[pl.ds(pl.multiple_of(source * 32, 32), 32), :])
        product = dot(
            jnp.concatenate([v_hi, v_lo, v_hi], axis=0), jnp.concatenate([r_hi, r_hi, r_lo], axis=0), 0, 0
        )
        if first:
            out[...] = product
        else:
            out[...] += product

    always = band >= 0

    def arrived(k):
        landed(always, lambda: f_copy(k))
        rotate(f_land[k], lax.rem(band + 3 - k, 4), k == 0)

    finish(0)
    start(always, lambda: f_copy(0))
    hand_on(2)
    finish(1)
    start(always, lambda: f_copy(1))
    finish(2)
    start(always, lambda: f_copy(2))
    hand_on(3)
    for k in range(3):
        arrived(k)
    finish(3)
    rotate(filt[:, pl.ds(lanes(band), QUARTER)], band, False)

    for k in range(4):
        sent(inner, lambda: y_all(k))
        sent(outer, lambda: y_outer(k))
        sent(outer, lambda: y_relay(k))
        for side in range(2):
            sent(exists[side] & x_used(side, k), lambda: x_copy(side, k))
    for side in range(2):
        sent(exists[4 + side], lambda: z_copy(side))
    for direction in range(6):
        sent(exists[direction], lambda: s_copy(direction))
        sent(exists[direction], lambda: c_copy(direction))
    for k in range(3):
        sent(always, lambda: f_copy(k))


def body(states, previous, potential, tile_atom, tile_cells, tile_count, projectors, coupling, rotation):
    vmem = pl.BlockSpec(memory_space=pltpu.VMEM)
    dma = pltpu.SemaphoreType.DMA
    operands = (
        states,
        previous,
        potential.reshape(1, -1),
        tile_atom.reshape(1, -1),
        tile_cells,
        projectors,
        coupling,
        rotation,
    )
    return pl.pallas_call(
        kernel,
        out_shape=jax.ShapeDtypeStruct((QUARTER, 128), F32),
        in_specs=[pl.BlockSpec(memory_space=pltpu.SMEM)] + [pl.BlockSpec(memory_space=pltpu.HBM)] * 8,
        out_specs=vmem,
        scratch_shapes=[
            *(pltpu.VMEM(operand.shape, operand.dtype) for operand in operands),
            dma((8,)),
            pltpu.VMEM((256, QUARTER), BF16),
            pltpu.VMEM((256, QUARTER), BF16),
            pltpu.VMEM((32, 4096), F32),
            pltpu.VMEM((2, 32, 4096), F32),
            pltpu.VMEM((2, 32, 4096), F32),
            pltpu.VMEM((2, 32, 4096), F32),
            pltpu.VMEM((2, 32, 512), F32),
            pltpu.VMEM((2, 32, 512), F32),
            pltpu.VMEM((6, 8, 128), F32),
            pltpu.VMEM((6, 8, 128), F32),
            pltpu.VMEM((8, 128), F32),
            pltpu.VMEM((6, 8, 128), F32),
            pltpu.VMEM((3, 32, QUARTER), F32),
            pltpu.VMEM((512, 4096), BF16),
            pltpu.VMEM((512, 4096), BF16),
            pltpu.VMEM((224, 512), BF16),
            dma((5, 4)),
            dma((5, 4)),
            dma((2, 4)),
            dma((2, 4)),
            dma((2,)),
            dma((2,)),
            dma((6,)),
            dma((6,)),
            dma((6,)),
            dma((6,)),
            dma((3,)),
            dma((3,)),
        ],
        compiler_params=pltpu.CompilerParams(
            collective_id=0, has_side_effects=True, vmem_limit_bytes=64 * 1024 * 1024
        ),
        name="chebyshev_step",
    )(tile_count, *operands)


def solution(mesh):
    placed = (
        P("band", "dom"),
        P("band", "dom"),
        P("dom"),
        P("dom"),
        P("dom", None),
        P("dom"),
        P("dom", None, None),
        P("dom", None, None),
        P(),
    )
    return jax.shard_map(
        body, mesh=mesh, in_specs=placed, out_specs=P(("dom", "band"), None), check_vma=False
    )
```

```python
import jax
import jax.numpy as jnp
from jax import lax
from jax.experimental import pallas as pl
from jax.experimental.pallas import tpu as pltpu
from jax.sharding import PartitionSpec as P

MESH = pl.DeviceIdType.MESH
F32 = jnp.float32
BF16 = jnp.bfloat16

STENCIL = (
    -5369.0 / 1800.0,
    12.0 / 7.0,
    -15.0 / 56.0,
    10.0 / 189.0,
    -1.0 / 112.0,
    2.0 / 1925.0,
    -1.0 / 16632.0,
)
W = tuple(-0.075 * w for w in STENCIL)
QUARTER = 1024
LINE = 512


def split(value):
    high = value.astype(BF16)
    return high, (value - high.astype(F32)).astype(BF16)


def faces_of(rows, columns):
    row = lax.broadcasted_iota(jnp.int32, (rows, 1), 0)
    column = lax.broadcasted_iota(jnp.int32, (rows, columns), 1)
    side, line, i = row // 128, (row // 8 & 15) * 64, row & 7
    used = i < 6
    cell = jnp.where(used, line + jnp.where(side == 0, 58 + i, i), -1)
    pick = jnp.where(column == cell, 1.0, 0.0).astype(BF16)
    face = jnp.zeros((rows, columns), F32)
    for n in range(1, 7):
        z = jnp.where(side == 0, n - 6 + i, 64 + i - n)
        place = jnp.where(used & (z >= 0) & (z < 64), line + z, -1)
        face = jnp.where(column == place, W[n], face)
    return pick, *split(face)


def inside_of(size):
    row = lax.broadcasted_iota(jnp.int32, (size, size), 0)
    column = lax.broadcasted_iota(jnp.int32, (size, size), 1)
    gap = jnp.where(row // 64 == column // 64, jnp.abs(row - column), 0)
    weight = jnp.zeros((size, size), F32)
    for n in range(1, 7):
        weight = jnp.where(gap == n, W[n], weight)
    return split(weight)


def dot(a, b, ca=1, cb=0):
    return lax.dot_general(a, b, (((ca,), (cb,)), ((), ())), preferred_element_type=F32)


def kernel(
    count_ref,
    states_in,
    previous_in,
    potential_in,
    atom_in,
    cells_in,
    projectors_in,
    coupling_in,
    rotation_in,
    out,
    states,
    previous,
    potential,
    tile_atom,
    tile_cells,
    projectors,
    coupling,
    rotation,
    load_sem,
    face_hi,
    face_lo,
    filt,
    y_land,
    x_send,
    x_land,
    z_send,
    z_land,
    s_send,
    s_land,
    c_send,
    c_land,
    f_land,
    t_send,
    t_land,
    turned_rotation,
    total_t,
    g_hi,
    g_lo,
    member,
    y_ss,
    y_rs,
    x_ss,
    x_rs,
    z_ss,
    z_rs,
    s_ss,
    s_rs,
    c_ss,
    c_rs,
    f_ss,
    f_rs,
    t_ss,
    t_rs,
):
    band = lax.axis_index("band")
    dom = lax.axis_index("dom")
    gz = lax.rem(dom, 4)
    gy = lax.rem(dom // 4, 4)
    gx = dom // 16
    steps = (16, -16, 4, -4, 1, -1)
    exists = (gx < 7, gx > 0, gy < 3, gy > 0, gz < 3, gz > 0)

    loads = [
        pltpu.make_async_copy(source, target, load_sem.at[n])
        for n, (source, target) in enumerate(
            (
                (states_in, states),
                (cells_in, tile_cells),
                (projectors_in, projectors),
                (atom_in, tile_atom),
                (previous_in, previous),
                (potential_in, potential),
                (coupling_in, coupling),
                (rotation_in, rotation),
            )
        )
    ]
    for load in loads:
        load.start()

    def there(direction):
        return (band, dom + steps[direction])

    def quarter_of(k):
        return lax.rem(band + 1 + k, 4)

    def lanes(quarter):
        return pl.multiple_of(quarter * QUARTER, QUARTER)

    def remote(source, target, sent, landed, device):
        return pltpu.make_async_remote_copy(
            src_ref=source,
            dst_ref=target,
            send_sem=sent,
            recv_sem=landed,
            device_id=device,
            device_id_type=MESH,
        )

    def start(needed, copies):
        @pl.when(needed)
        def _():
            for copy in copies():
                copy.start()

    def landed(needed, copies):
        @pl.when(needed)
        def _():
            for copy in copies():
                copy.wait_recv()

    def sent(needed, copies):
        @pl.when(needed)
        def _():
            for copy in copies():
                copy.wait_send()

    outer = (gy == 0) | (gy == 3)
    inner = jnp.logical_not(outer)
    even = lax.rem(gy, 2) == 0
    partner = (band, jnp.where(even, dom + 4, dom - 4))
    far = (band, jnp.where(gy < 2, dom + 8, dom - 8))
    partner_side = jnp.where(even, 1, 0)
    six = jnp.where(gy == 0, 128, 0)

    barrier = pltpu.get_barrier_semaphore()
    for direction in range(6):

        @pl.when(exists[direction])
        def _():
            pl.semaphore_signal(barrier, inc=1, device_id=there(direction), device_id_type=MESH)

    for other in range(1, 4):
        pl.semaphore_signal(
            barrier, inc=1, device_id=(lax.rem(band + other, 4), dom), device_id_type=MESH
        )
    pl.semaphore_signal(barrier, inc=1, device_id=far, device_id_type=MESH)
    partners = 4
    for direction in range(6):
        partners = partners + jnp.where(exists[direction], 1, 0)
    pl.semaphore_wait(barrier, partners)

    def y_all(k):
        block = pl.ds(lanes(quarter_of(k)), QUARTER)
        return [
            remote(states_in.at[:, block], y_land.at[1 - partner_side, :, block], y_ss.at[0, k], y_rs.at[0, k], partner)
        ]

    def y_six(source, number, k, device):
        copies = []
        for i in range(2):
            block = pl.ds(pl.multiple_of(lanes(quarter_of(k)) + i * LINE + six, 128), 384)
            copies.append(
                remote(
                    source.at[:, block],
                    y_land.at[1 - partner_side, :, block],
                    y_ss.at[number + i, k],
                    y_rs.at[number + i, k],
                    device,
                )
            )
        return copies

    def y_outer(k):
        return y_six(states_in, 1, k, partner)

    def y_relay(k):
        return y_six(y_land.at[partner_side], 3, k, far)

    def y_start(k):
        start(inner, lambda: y_all(k))
        start(outer, lambda: y_outer(k))

    def hand_on(k):
        landed(outer, lambda: y_all(k))
        start(outer, lambda: y_relay(k))

    def x_copy(side, k):
        block = pl.ds(lanes(quarter_of(k)), QUARTER)
        return [
            remote(
                x_send.at[side, :, block], x_land.at[side, :, block], x_ss.at[side, k], x_rs.at[side, k], there(side)
            )
        ]

    def x_used(side, k):
        return quarter_of(k) < 3 if side == 0 else quarter_of(k) > 0

    def x_start(k):
        for side in range(2):
            start(exists[side] & x_used(side, k), lambda: x_copy(side, k))

    def z_copy(side):
        return [remote(z_send.at[side], z_land.at[side], z_ss.at[side], z_rs.at[side], there(4 + side))]

    def s_copy(direction):
        return [
            remote(
                s_send.at[direction], s_land.at[direction], s_ss.at[direction], s_rs.at[direction], there(direction)
            )
        ]

    def c_copy(direction):
        return [remote(c_send, c_land.at[direction], c_ss.at[direction], c_rs.at[direction], there(direction))]

    def f_copy(k):
        return [
            remote(
                filt.at[:, pl.ds(lanes(quarter_of(k)), QUARTER)],
                f_land.at[k],
                f_ss.at[k],
                f_rs.at[k],
                (quarter_of(k), dom),
            )
        ]

    def t_copy(i):
        return [remote(t_send, t_land.at[i], t_ss.at[i], t_rs.at[i], (lax.rem(band + 1 + i, 4), dom))]

    always = band >= 0

    y_start(0)

    def x_parts(g, _):
        rows = pl.ds(pl.multiple_of(g * 8, 8), 8)
        for column in range(4):
            layer = [states[rows, pl.ds(x * LINE + column * 128, 128)] for x in range(8)]
            for target in range(6):
                total = W[6] * layer[target + 2]
                for m in range(target + 3, 8):
                    total = total + W[target + 8 - m] * layer[m]
                x_send[0, rows, pl.ds(target * LINE + column * 128, 128)] = total
            for target in range(2, 8):
                total = W[6] * layer[target - 2]
                for m in range(target - 2):
                    total = total + W[m + 8 - target] * layer[m]
                x_send[1, rows, pl.ds(target * LINE + column * 128, 128)] = total
        return 0

    loads[0].wait()
    lax.fori_loop(0, 4, x_parts, 0)
    x_start(0)

    pick, *face = faces_of(256, QUARTER)
    face_hi[...], face_lo[...] = face
    pieces = []
    for quarter in range(4):
        pieces.extend(split(states[:, pl.ds(quarter * QUARTER, QUARTER)]))
    picked = dot(jnp.concatenate(pieces, axis=0), pick, 1, 1)
    for quarter in range(4):
        both = picked[quarter * 64 : quarter * 64 + 32] + picked[quarter * 64 + 32 : quarter * 64 + 64]
        z_send[0, :, pl.ds(quarter * 128, 128)] = both[:, 0:128]
        z_send[1, :, pl.ds(quarter * 128, 128)] = both[:, 128:256]

    for side in range(2):
        start(exists[4 + side], lambda: z_copy(side))

        @pl.when(jnp.logical_not(exists[5 - side]))
        def _():
            z_land[side] = jnp.zeros((32, 512), F32)

        @pl.when(jnp.logical_not(exists[3 - side]))
        def _():
            y_land[side] = jnp.zeros((32, 4096), F32)

    for direction in range(6):

        @pl.when(jnp.logical_not(exists[direction ^ 1]))
        def _():
            s_land[direction] = jnp.zeros((8, 128), F32)
            c_land[direction] = jnp.zeros((8, 128), F32)

    loads[1].wait()
    loads[2].wait()

    low_row = lax.broadcasted_iota(jnp.int32, (256, 128), 0).astype(F32).astype(BF16)
    high_row = (lax.broadcasted_iota(jnp.int32, (16, 128), 0) // 8).astype(F32).astype(BF16)
    high_rows = [high_row + jnp.asarray(2 * h, BF16) for h in range(8)]
    zero, one = jnp.asarray(0, BF16), jnp.asarray(1, BF16)

    def tile_pair(pair, _):
        spread = []
        for which in range(2):
            t = pair * 2 + which
            cells = tile_cells[pl.ds(t, 1), :]
            high = jnp.broadcast_to((cells >> 8).astype(F32), (16, 128)).astype(BF16)
            low = jnp.broadcast_to((cells & 255).astype(F32), (16, 128)).astype(BF16)
            low = jnp.concatenate([low] * 16, axis=0)
            w = projectors[t]
            w_hi = w.astype(BF16).astype(F32)
            w_lo = w - w_hi
            w_hi = jnp.concatenate([w_hi, w_hi], axis=0).astype(BF16)
            w_lo = jnp.concatenate([w_lo, w_lo], axis=0).astype(BF16)
            here = [high == row for row in high_rows]
            left = jnp.concatenate(
                [
                    jnp.concatenate([jnp.where(mask, w_hi, zero) for mask in here], axis=0),
                    jnp.concatenate([jnp.where(mask, w_lo, zero) for mask in here], axis=0),
                ],
                axis=1,
            )
            hot = jnp.where(low_row == low, one, zero)
            spread.append(dot(left, jnp.concatenate([hot, hot], axis=1), 1, 1))
        rows = pl.ds(pl.multiple_of(pair * 16, 16), 16)
        for h in range(16):
            both = jnp.concatenate([spread[0][h * 8 : h * 8 + 8], spread[1][h * 8 : h * 8 + 8]], axis=0)
            both_hi, both_lo = split(both)
            g_hi[rows, pl.ds(h * 256, 256)] = both_hi
            g_lo[rows, pl.ds(h * 256, 256)] = both_lo
        return 0

    lax.fori_loop(0, 32, tile_pair, 0, unroll=4)

    loads[3].wait()
    relative = (tile_atom[...] - dom * 4).astype(F32).astype(BF16)
    repeat = (
        lax.broadcasted_iota(jnp.int32, (64, 512), 0) == lax.broadcasted_iota(jnp.int32, (64, 512), 1) // 8
    )
    owner = dot(
        jnp.broadcast_to(relative.astype(F32), (16, 64)).astype(BF16), jnp.where(repeat, 1.0, 0.0).astype(BF16)
    )[0:1]
    slot = lax.broadcasted_iota(jnp.int32, (1, 512), 1)
    owner = jnp.where(slot // 8 < count_ref[0], owner, 1000.0)
    row = lax.broadcasted_iota(jnp.int32, (32, 512), 0)
    same_j = (row & 7) == (lax.broadcasted_iota(jnp.int32, (32, 512), 1) & 7)
    atom = (row // 8).astype(F32)
    for number, step in enumerate((0,) + steps):
        match = same_j & (atom + 4.0 * step == owner)
        member[pl.ds(number * 32, 32), :] = jnp.where(match, 1.0, 0.0).astype(BF16)

    st_hi, st_lo = split(states[...])
    partial_hi = dot(g_hi[...], jnp.concatenate([st_hi, st_lo], axis=0), 1, 1)
    partial_value = partial_hi[:, 0:32] + partial_hi[:, 32:64] + dot(g_lo[...], st_hi, 1, 1)
    part_hi, part_lo = split(partial_value)
    sums = dot(member[...], part_hi) + dot(member[...], part_lo)
    messages = []
    for number in range(7):
        messages.append(
            jnp.concatenate([sums[number * 32 + a * 8 : number * 32 + a * 8 + 8] for a in range(4)], axis=1)
        )
    for direction in range(6):
        s_send[direction] = messages[direction + 1]
    for direction in range(6):
        start(exists[direction], lambda: s_copy(direction))
    y_start(1)
    x_start(1)

    def base(g, _):
        rows = pl.ds(pl.multiple_of(g * 8, 8), 8)
        for column in range(4):
            layer = [states[rows, pl.ds(x * LINE + column * 128, 128)] for x in range(8)]
            for x in range(8):
                block = pl.ds(x * LINE + column * 128, 128)
                total = layer[x] * (3.0 * W[0] - 1.2 + 0.15 * potential[:, block]) - 0.3 * previous[rows, block]
                for k in range(1, 7):
                    pair = [layer[m] for m in (x - k, x + k) if 0 <= m < 8]
                    if pair:
                        total = total + W[k] * (pair[0] + pair[1] if len(pair) == 2 else pair[0])
                filt[rows, block] = total
        return 0

    for n in (4, 5):
        loads[n].wait()
    lax.fori_loop(0, 4, base, 0)
    blocks = [states[:, pl.ds(i * 256, 256)] for i in range(16)]
    tall_hi, tall_lo = split(jnp.concatenate(blocks, axis=0))
    in_hi, in_lo = inside_of(256)
    inside = dot(tall_hi, in_hi) + dot(tall_lo, in_hi) + dot(tall_hi, in_lo)
    for i in range(16):
        filt[:, pl.ds(i * 256, 256)] += inside[i * 32 : i * 32 + 32]

    loads[7].wait()
    order = [rotation[pl.ds(pl.multiple_of(lax.rem(band + i, 4) * 32, 32), 32), :] for i in range(4)]
    order = jnp.concatenate(order, axis=0)
    order_hi, order_lo = split(order)
    across_hi, across_lo = split(order.T)
    for i in range(4):
        part = slice(i * 32, i * 32 + 32)
        turned_rotation[i] = jnp.concatenate([across_hi[:, part], across_hi[:, part], across_lo[:, part]], axis=1)

    hand_on(0)

    for side in range(2):
        landed(exists[5 - side], lambda: z_copy(side))
    faces = []
    for quarter in range(4):
        block = pl.ds(quarter * 128, 128)
        faces.append(jnp.concatenate([z_land[0, :, block], z_land[1, :, block]], axis=1))
    faces_hi, faces_lo = split(jnp.concatenate(faces, axis=0))
    edge = dot(faces_hi, face_hi[...]) + dot(faces_lo, face_hi[...]) + dot(faces_hi, face_lo[...])
    for quarter in range(4):
        filt[:, pl.ds(quarter * QUARTER, QUARTER)] += edge[quarter * 32 : quarter * 32 + 32]

    loads[6].wait()
    lane = lax.broadcasted_iota(jnp.int32, (8, 128), 1) // 32
    mixing = []
    for j in range(8):
        column = jnp.zeros((8, 128), F32)
        for a in range(4):
            column = jnp.where(lane == a, coupling[a][:, j : j + 1], column)
        mixing.append(column)
    owned = messages[0]
    for direction in range(6):
        landed(exists[direction ^ 1], lambda: s_copy(direction))
        owned = owned + s_land[direction]
    coef = mixing[0] * owned[0:1, :]
    for j in range(1, 8):
        coef = coef + mixing[j] * owned[j : j + 1, :]
    c_send[...] = coef
    t_send[:, 0:128] = coef
    for direction in range(6):
        start(exists[direction], lambda: c_copy(direction))
    y_start(2)
    x_start(2)

    left_half = lax.broadcasted_iota(jnp.int32, (8, 128), 1) < 64

    def finish(k):
        quarter = quarter_of(k)
        for side in range(2):

            @pl.when(exists[side ^ 1] & x_used(side, k))
            def _():
                x_copy(side, k)[0].wait_recv()
                block = pl.ds(lanes(quarter), QUARTER)
                filt[:, block] += x_land[side, :, block]

        landed(inner, lambda: y_outer(k))
        landed(inner, lambda: y_relay(k))

        def line(n, _):
            rows = pl.ds(pl.multiple_of(lax.rem(n, 4) * 8, 8), 8)
            begin = lanes(quarter) + n // 4 * LINE

            def at(offset):
                return pl.ds(pl.multiple_of(begin + offset, 128), 128)

            run = [y_land[0, rows, at(128 + 128 * i)] for i in range(3)]
            run += [states[rows, at(128 * i)] for i in range(4)]
            run += [y_land[1, rows, at(128 * i)] for i in range(3)]
            turned = [pltpu.roll(v, 64, 1) for v in run]
            odd = []
            for g in range(3, 8):
                odd.append(
                    W[1] * (turned[g] + turned[g - 1])
                    + W[3] * (turned[min(g + 1, 9)] + turned[g - 2])
                    + W[5] * (turned[min(g + 2, 9)] + turned[g - 3])
                )
            for g in range(4):
                total = filt[rows, at(128 * g)]
                for n_far in (2, 4, 6):
                    total = total + W[n_far] * (run[g + 3 + n_far // 2] + run[g + 3 - n_far // 2])
                filt[rows, at(128 * g)] = total + jnp.where(left_half, odd[g], odd[g + 1])
            return 0

        lax.fori_loop(0, 8, line, 0, unroll=8)

    def rotated(value, i):
        high, low = split(value)
        return dot(turned_rotation[i], jnp.concatenate([high, low, high], axis=0))

    def arrived(k):
        landed(always, lambda: f_copy(k))
        total_t[...] += rotated(f_land[k], 3 - k)

    finish(0)
    start(always, lambda: f_copy(0))
    hand_on(1)

    for direction in range(6):
        landed(exists[direction ^ 1], lambda: c_copy(direction))
    for direction in range(6):
        t_send[:, pl.ds((direction + 1) * 128, 128)] = c_land[direction ^ 1]
    for i in range(3):
        start(always, lambda: t_copy(i))
    y_start(3)
    x_start(3)
    finish(1)
    start(always, lambda: f_copy(1))
    hand_on(2)

    tables = [t_send]
    for i in range(3):
        landed(always, lambda: t_copy(i))
    tables += [t_land.at[2 - i] for i in range(3)]
    known = []
    for group in range(28):
        known.append(jnp.concatenate([table[:, group * 32 : group * 32 + 32] for table in tables], axis=1))
    known_hi, known_lo = split(jnp.concatenate(known, axis=0))
    mixed = 0.15 * (dot(known_hi, order_hi) + dot(known_lo, order_hi) + dot(known_hi, order_lo))
    of_tile = dot(jnp.concatenate(split(mixed.T), axis=0), member[...]).astype(BF16)
    mine = pl.ds(lanes(band), QUARTER)
    nonlocal_t = dot(of_tile, g_hi[:, mine])
    total_t[...] = nonlocal_t[0:128] + nonlocal_t[128:256] + dot(of_tile[0:128], g_lo[:, mine])

    arrived(0)
    finish(2)
    start(always, lambda: f_copy(2))
    arrived(1)
    hand_on(3)
    arrived(2)
    finish(3)
    out[...] = (total_t[...] + rotated(filt[:, mine], 0)).T

    for k in range(4):
        sent(inner, lambda: y_all(k))
        sent(outer, lambda: y_outer(k))
        sent(outer, lambda: y_relay(k))
        for side in range(2):
            sent(exists[side] & x_used(side, k), lambda: x_copy(side, k))
    for side in range(2):
        sent(exists[4 + side], lambda: z_copy(side))
    for direction in range(6):
        sent(exists[direction], lambda: s_copy(direction))
        sent(exists[direction], lambda: c_copy(direction))
    for k in range(3):
        sent(always, lambda: f_copy(k))
        sent(always, lambda: t_copy(k))


def body(states, previous, potential, tile_atom, tile_cells, tile_count, projectors, coupling, rotation):
    vmem = pl.BlockSpec(memory_space=pltpu.VMEM)
    dma = pltpu.SemaphoreType.DMA
    operands = (
        states,
        previous,
        potential.reshape(1, -1),
        tile_atom.reshape(1, -1),
        tile_cells,
        projectors,
        coupling,
        rotation,
    )
    return pl.pallas_call(
        kernel,
        out_shape=jax.ShapeDtypeStruct((QUARTER, 128), F32),
        in_specs=[pl.BlockSpec(memory_space=pltpu.SMEM)] + [pl.BlockSpec(memory_space=pltpu.HBM)] * 8,
        out_specs=vmem,
        scratch_shapes=[
            *(pltpu.VMEM(operand.shape, operand.dtype) for operand in operands),
            dma((8,)),
            pltpu.VMEM((256, QUARTER), BF16),
            pltpu.VMEM((256, QUARTER), BF16),
            pltpu.VMEM((32, 4096), F32),
            pltpu.VMEM((2, 32, 4096), F32),
            pltpu.VMEM((2, 32, 4096), F32),
            pltpu.VMEM((2, 32, 4096), F32),
            pltpu.VMEM((2, 32, 512), F32),
            pltpu.VMEM((2, 32, 512), F32),
            pltpu.VMEM((6, 8, 128), F32),
            pltpu.VMEM((6, 8, 128), F32),
            pltpu.VMEM((8, 128), F32),
            pltpu.VMEM((6, 8, 128), F32),
            pltpu.VMEM((3, 32, QUARTER), F32),
            pltpu.VMEM((8, 896), F32),
            pltpu.VMEM((3, 8, 896), F32),
            pltpu.VMEM((4, 128, 96), BF16),
            pltpu.VMEM((128, QUARTER), F32),
            pltpu.VMEM((512, 4096), BF16),
            pltpu.VMEM((512, 4096), BF16),
            pltpu.VMEM((224, 512), BF16),
            dma((5, 4)),
            dma((5, 4)),
            dma((2, 4)),
            dma((2, 4)),
            dma((2,)),
            dma((2,)),
            dma((6,)),
            dma((6,)),
            dma((6,)),
            dma((6,)),
            dma((3,)),
            dma((3,)),
            dma((3,)),
            dma((3,)),
        ],
        compiler_params=pltpu.CompilerParams(
            collective_id=0, has_side_effects=True, vmem_limit_bytes=64 * 1024 * 1024
        ),
        name="chebyshev_step",
    )(tile_count, *operands)


def solution(mesh):
    placed = (
        P("band", "dom"),
        P("band", "dom"),
        P("dom"),
        P("dom"),
        P("dom", None),
        P("dom"),
        P("dom", None, None),
        P("dom", None, None),
        P(),
    )
    return jax.shard_map(
        body, mesh=mesh, in_specs=placed, out_specs=P(("dom", "band"), None), check_vma=False
    )
```

```python
import jax
import jax.numpy as jnp
from jax import lax
from jax.experimental import pallas as pl
from jax.experimental.pallas import tpu as pltpu
from jax.sharding import PartitionSpec as P

MESH = pl.DeviceIdType.MESH
F32 = jnp.float32
BF16 = jnp.bfloat16

STENCIL = (
    -5369.0 / 1800.0,
    12.0 / 7.0,
    -15.0 / 56.0,
    10.0 / 189.0,
    -1.0 / 112.0,
    2.0 / 1925.0,
    -1.0 / 16632.0,
)
W = tuple(-0.075 * w for w in STENCIL)
QUARTER = 1024
LINE = 512


def split(value):
    high = value.astype(BF16)
    return high, (value - high.astype(F32)).astype(BF16)


def faces_of(rows, columns):
    row = lax.broadcasted_iota(jnp.int32, (rows, 1), 0)
    column = lax.broadcasted_iota(jnp.int32, (rows, columns), 1)
    side, line, i = row // 128, (row // 8 & 15) * 64, row & 7
    used = i < 6
    cell = jnp.where(used, line + jnp.where(side == 0, 58 + i, i), -1)
    pick = jnp.where(column == cell, 1.0, 0.0).astype(BF16)
    face = jnp.zeros((rows, columns), F32)
    for n in range(1, 7):
        z = jnp.where(side == 0, n - 6 + i, 64 + i - n)
        place = jnp.where(used & (z >= 0) & (z < 64), line + z, -1)
        face = jnp.where(column == place, W[n], face)
    return pick, *split(face)


def inside_of(size):
    row = lax.broadcasted_iota(jnp.int32, (size, size), 0)
    column = lax.broadcasted_iota(jnp.int32, (size, size), 1)
    gap = jnp.where(row // 64 == column // 64, jnp.abs(row - column), 0)
    weight = jnp.zeros((size, size), F32)
    for n in range(1, 7):
        weight = jnp.where(gap == n, W[n], weight)
    return split(weight)


def dot(a, b, ca=1, cb=0):
    return lax.dot_general(a, b, (((ca,), (cb,)), ((), ())), preferred_element_type=F32)


def kernel(
    count_ref,
    states_in,
    previous_in,
    potential_in,
    atom_in,
    cells_in,
    projectors_in,
    coupling_in,
    rotation_in,
    out,
    states,
    previous,
    potential,
    tile_atom,
    tile_cells,
    projectors,
    coupling,
    rotation,
    load_sem,
    face_hi,
    face_lo,
    filt,
    y_land,
    aside,
    x_send,
    x_land,
    z_send,
    z_land,
    s_send,
    s_land,
    c_send,
    c_land,
    f_land,
    t_send,
    t_land,
    turned_rotation,
    total_t,
    g_hi,
    g_lo,
    member,
    y_ss,
    y_rs,
    x_ss,
    x_rs,
    z_ss,
    z_rs,
    s_ss,
    s_rs,
    c_ss,
    c_rs,
    f_ss,
    f_rs,
    t_ss,
    t_rs,
    ready,
):
    band = lax.axis_index("band")
    dom = lax.axis_index("dom")
    gz = lax.rem(dom, 4)
    gy = lax.rem(dom // 4, 4)
    gx = dom // 16
    steps = (16, -16, 4, -4, 1, -1)
    exists = (gx < 7, gx > 0, gy < 3, gy > 0, gz < 3, gz > 0)

    loads = [
        pltpu.make_async_copy(source, target, load_sem.at[n])
        for n, (source, target) in enumerate(
            (
                (states_in, states),
                (cells_in, tile_cells),
                (projectors_in, projectors),
                (atom_in, tile_atom),
                (previous_in, previous),
                (potential_in, potential),
                (coupling_in, coupling),
                (rotation_in, rotation),
            )
        )
    ]
    for load in loads:
        load.start()

    always = band >= 0

    def there(direction):
        return (band, dom + steps[direction])

    def quarter_of(k):
        return lax.rem(band + 1 + k, 4)

    def lanes(quarter):
        return pl.multiple_of(quarter * QUARTER, QUARTER)

    def remote(source, target, sent, landed, device):
        return pltpu.make_async_remote_copy(
            src_ref=source,
            dst_ref=target,
            send_sem=sent,
            recv_sem=landed,
            device_id=device,
            device_id_type=MESH,
        )

    def start(needed, copies):
        @pl.when(needed)
        def _():
            for copy in copies():
                copy.start()

    def landed(needed, copies):
        @pl.when(needed)
        def _():
            for copy in copies():
                copy.wait_recv()

    def sent(needed, copies):
        @pl.when(needed)
        def _():
            for copy in copies():
                copy.wait_send()

    outer = (gy == 0) | (gy == 3)
    inner = jnp.logical_not(outer)
    even = lax.rem(gy, 2) == 0
    partner = (band, jnp.where(even, dom + 4, dom - 4))
    far = (band, jnp.where(gy < 2, dom + 8, dom - 8))
    partner_side = jnp.where(even, 1, 0)
    near_six = jnp.where(even, 128, 0)
    far_six = 128 - near_six

    later = (exists[0] & (gx != 3), exists[1] & (gx == 4))
    earlier = (exists[0] & (gx == 3), exists[1] & (gx != 4))
    barrier = pltpu.get_barrier_semaphore()
    for direction in range(6):

        @pl.when(later[direction] if direction < 2 else exists[direction])
        def _():
            pl.semaphore_signal(barrier, inc=1, device_id=there(direction), device_id_type=MESH)

    for other in range(1, 4):
        pl.semaphore_signal(
            barrier, inc=1, device_id=(lax.rem(band + other, 4), dom), device_id_type=MESH
        )
    pl.semaphore_signal(barrier, inc=1, device_id=far, device_id_type=MESH)
    partners = 4
    for direction in range(6):
        partners = partners + jnp.where(earlier[direction] if direction < 2 else exists[direction], 1, 0)
    pl.semaphore_wait(barrier, partners)
    for side in range(2):

        @pl.when(earlier[side])
        def _():
            pl.semaphore_signal(ready.at[1 - side], inc=1, device_id=there(side), device_id_type=MESH)

    def later_ready():
        for side in range(2):

            @pl.when(later[side])
            def _():
                pl.semaphore_wait(ready.at[side], 1)

    def half(m):
        return pl.ds(m % 2 * 16, 16)

    def y_all(m):
        block = pl.ds(lanes(quarter_of(m // 2)), QUARTER)
        return [
            remote(
                states_in.at[half(m), block],
                y_land.at[1 - partner_side, half(m), block],
                y_ss.at[0, m],
                y_rs.at[0, m],
                partner,
            )
        ]

    def y_six(m, source, source_start, target, target_start, six, number, device):
        copies = []
        for i in range(2):
            here = pl.ds(pl.multiple_of(source_start + i * LINE + six, 128), 384)
            over_there = pl.ds(pl.multiple_of(target_start + i * LINE + six, 128), 384)
            copies.append(
                remote(
                    source.at[half(m), here],
                    target.at[half(m), over_there],
                    y_ss.at[number + i, m],
                    y_rs.at[number + i, m],
                    device,
                )
            )
        return copies

    def y_near(m):
        begin = lanes(quarter_of(m // 2))
        return y_six(m, states_in, begin, y_land.at[1 - partner_side], begin, near_six, 1, partner)

    def y_relay(m):
        begin = lanes(quarter_of(m // 2))
        return y_six(m, y_land.at[partner_side], begin, y_land.at[1 - partner_side], begin, near_six, 3, far)

    def y_aside(m):
        return y_six(m, states_in, lanes(quarter_of(3)), aside, 0, far_six, 5, far)

    def y_back(m):
        return y_six(m, aside, 0, y_land.at[partner_side], lanes(quarter_of(3)), far_six, 3, partner)

    def y_start(m):
        if m < 6:
            start(inner, lambda: y_all(m))
            start(outer, lambda: y_near(m))
        else:
            start(always, lambda: y_near(m))

    def hand_on(k):
        for m in (2 * k, 2 * k + 1):
            if k < 3:
                landed(outer, lambda: y_all(m))
                start(outer, lambda: y_relay(m))
            else:
                landed(outer, lambda: y_aside(m))
                start(outer, lambda: y_back(m))

    def y_landed(k):
        for m in (2 * k, 2 * k + 1):
            if k < 3:
                landed(inner, lambda: y_near(m))
                landed(inner, lambda: y_relay(m))
            else:
                landed(always, lambda: y_near(m))
                landed(inner, lambda: y_back(m))

    def x_copy(side, m):
        block = pl.ds(lanes(quarter_of(m // 2)), QUARTER)
        return [
            remote(
                x_send.at[side, half(m), block],
                x_land.at[side, half(m), block],
                x_ss.at[side, m],
                x_rs.at[side, m],
                there(side),
            )
        ]

    def x_used(side, k):
        return quarter_of(k) < 3 if side == 0 else quarter_of(k) > 0

    def x_start(m, to=exists):
        for side in range(2):
            start(to[side] & x_used(side, m // 2), lambda: x_copy(side, m))

    def z_copy(side):
        return [remote(z_send.at[side], z_land.at[side], z_ss.at[side], z_rs.at[side], there(4 + side))]

    def s_copy(direction):
        return [
            remote(
                s_send.at[direction], s_land.at[direction], s_ss.at[direction], s_rs.at[direction], there(direction)
            )
        ]

    def c_copy(direction):
        return [remote(c_send, c_land.at[direction], c_ss.at[direction], c_rs.at[direction], there(direction))]

    def f_copy(k):
        return [
            remote(
                filt.at[:, pl.ds(lanes(quarter_of(k)), QUARTER)],
                f_land.at[k],
                f_ss.at[k],
                f_rs.at[k],
                (quarter_of(k), dom),
            )
        ]

    def t_copy(i):
        return [remote(t_send, t_land.at[i], t_ss.at[i], t_rs.at[i], (lax.rem(band + 1 + i, 4), dom))]

    y_start(0)
    y_start(1)
    y_start(2)
    for m in (6, 7):
        start(inner, lambda: y_aside(m))

    def x_parts(g, _):
        rows = pl.ds(pl.multiple_of(g * 8, 8), 8)
        for column in range(4):
            layer = [states[rows, pl.ds(x * LINE + column * 128, 128)] for x in range(8)]
            for target in range(6):
                total = W[6] * layer[target + 2]
                for m in range(target + 3, 8):
                    total = total + W[target + 8 - m] * layer[m]
                x_send[0, rows, pl.ds(target * LINE + column * 128, 128)] = total
            for target in range(2, 8):
                total = W[6] * layer[target - 2]
                for m in range(target - 2):
                    total = total + W[m + 8 - target] * layer[m]
                x_send[1, rows, pl.ds(target * LINE + column * 128, 128)] = total
        return 0

    loads[0].wait()
    lax.fori_loop(0, 4, x_parts, 0)
    x_start(0, earlier)
    x_start(1, earlier)
    x_start(2, earlier)

    pick, *face = faces_of(256, QUARTER)
    face_hi[...], face_lo[...] = face
    pieces = []
    for quarter in range(4):
        pieces.extend(split(states[:, pl.ds(quarter * QUARTER, QUARTER)]))
    picked = dot(jnp.concatenate(pieces, axis=0), pick, 1, 1)
    for quarter in range(4):
        both = picked[quarter * 64 : quarter * 64 + 32] + picked[quarter * 64 + 32 : quarter * 64 + 64]
        z_send[0, :, pl.ds(quarter * 128, 128)] = both[:, 0:128]
        z_send[1, :, pl.ds(quarter * 128, 128)] = both[:, 128:256]

    for side in range(2):
        start(exists[4 + side], lambda: z_copy(side))

        @pl.when(jnp.logical_not(exists[5 - side]))
        def _():
            z_land[side] = jnp.zeros((32, 512), F32)

        @pl.when(jnp.logical_not(exists[3 - side]))
        def _():
            y_land[side] = jnp.zeros((32, 4096), F32)

    for direction in range(6):

        @pl.when(jnp.logical_not(exists[direction ^ 1]))
        def _():
            s_land[direction] = jnp.zeros((8, 128), F32)
            c_land[direction] = jnp.zeros((8, 128), F32)

    loads[1].wait()
    loads[2].wait()

    low_row = lax.broadcasted_iota(jnp.int32, (256, 128), 0).astype(F32).astype(BF16)
    high_row = (lax.broadcasted_iota(jnp.int32, (16, 128), 0) // 8).astype(F32).astype(BF16)
    high_rows = [high_row + jnp.asarray(2 * h, BF16) for h in range(8)]
    zero, one = jnp.asarray(0, BF16), jnp.asarray(1, BF16)

    def tile_pair(pair, _):
        spread = []
        for which in range(2):
            t = pair * 2 + which
            cells = tile_cells[pl.ds(t, 1), :]
            high = jnp.broadcast_to((cells >> 8).astype(F32), (16, 128)).astype(BF16)
            low = jnp.broadcast_to((cells & 255).astype(F32), (16, 128)).astype(BF16)
            low = jnp.concatenate([low] * 16, axis=0)
            w = projectors[t]
            w_hi = w.astype(BF16).astype(F32)
            w_lo = w - w_hi
            w_hi = jnp.concatenate([w_hi, w_hi], axis=0).astype(BF16)
            w_lo = jnp.concatenate([w_lo, w_lo], axis=0).astype(BF16)
            here = [high == row for row in high_rows]
            left = jnp.concatenate(
                [
                    jnp.concatenate([jnp.where(mask, w_hi, zero) for mask in here], axis=0),
                    jnp.concatenate([jnp.where(mask, w_lo, zero) for mask in here], axis=0),
                ],
                axis=1,
            )
            hot = jnp.where(low_row == low, one, zero)
            spread.append(dot(left, jnp.concatenate([hot, hot], axis=1), 1, 1))
        rows = pl.ds(pl.multiple_of(pair * 16, 16), 16)
        for h in range(16):
            both = jnp.concatenate([spread[0][h * 8 : h * 8 + 8], spread[1][h * 8 : h * 8 + 8]], axis=0)
            both_hi, both_lo = split(both)
            g_hi[rows, pl.ds(h * 256, 256)] = both_hi
            g_lo[rows, pl.ds(h * 256, 256)] = both_lo
        return 0

    lax.fori_loop(0, 16, tile_pair, 0, unroll=4)
    later_ready()
    x_start(0, later)
    x_start(1, later)
    x_start(2, later)
    lax.fori_loop(16, 32, tile_pair, 0, unroll=4)

    loads[3].wait()
    relative = (tile_atom[...] - dom * 4).astype(F32).astype(BF16)
    repeat = (
        lax.broadcasted_iota(jnp.int32, (64, 512), 0) == lax.broadcasted_iota(jnp.int32, (64, 512), 1) // 8
    )
    owner = dot(
        jnp.broadcast_to(relative.astype(F32), (16, 64)).astype(BF16), jnp.where(repeat, 1.0, 0.0).astype(BF16)
    )[0:1]
    slot = lax.broadcasted_iota(jnp.int32, (1, 512), 1)
    owner = jnp.where(slot // 8 < count_ref[0], owner, 1000.0)
    row = lax.broadcasted_iota(jnp.int32, (32, 512), 0)
    same_j = (row & 7) == (lax.broadcasted_iota(jnp.int32, (32, 512), 1) & 7)
    atom = (row // 8).astype(F32)
    for number, step in enumerate((0,) + steps):
        match = same_j & (atom + 4.0 * step == owner)
        member[pl.ds(number * 32, 32), :] = jnp.where(match, 1.0, 0.0).astype(BF16)

    st_hi, st_lo = split(states[...])
    partial_hi = dot(g_hi[...], jnp.concatenate([st_hi, st_lo], axis=0), 1, 1)
    partial_value = partial_hi[:, 0:32] + partial_hi[:, 32:64] + dot(g_lo[...], st_hi, 1, 1)
    part_hi, part_lo = split(partial_value)
    sums = dot(member[...], part_hi) + dot(member[...], part_lo)
    messages = []
    for number in range(7):
        messages.append(
            jnp.concatenate([sums[number * 32 + a * 8 : number * 32 + a * 8 + 8] for a in range(4)], axis=1)
        )
    for direction in range(6):
        s_send[direction] = messages[direction + 1]
    for direction in range(6):
        start(exists[direction], lambda: s_copy(direction))
    y_start(3)
    y_start(4)
    x_start(3)
    x_start(4)
    hand_on(3)

    def base(g, _):
        rows = pl.ds(pl.multiple_of(g * 8, 8), 8)
        for column in range(4):
            layer = [states[rows, pl.ds(x * LINE + column * 128, 128)] for x in range(8)]
            for x in range(8):
                block = pl.ds(x * LINE + column * 128, 128)
                total = layer[x] * (3.0 * W[0] - 1.2 + 0.15 * potential[:, block]) - 0.3 * previous[rows, block]
                for k in range(1, 7):
                    pair = [layer[m] for m in (x - k, x + k) if 0 <= m < 8]
                    if pair:
                        total = total + W[k] * (pair[0] + pair[1] if len(pair) == 2 else pair[0])
                filt[rows, block] = total
        return 0

    for n in (4, 5):
        loads[n].wait()
    lax.fori_loop(0, 4, base, 0)
    blocks = [states[:, pl.ds(i * 256, 256)] for i in range(16)]
    tall_hi, tall_lo = split(jnp.concatenate(blocks, axis=0))
    in_hi, in_lo = inside_of(256)
    inside = dot(tall_hi, in_hi) + dot(tall_lo, in_hi) + dot(tall_hi, in_lo)
    for i in range(16):
        filt[:, pl.ds(i * 256, 256)] += inside[i * 32 : i * 32 + 32]

    loads[7].wait()
    order = [rotation[pl.ds(pl.multiple_of(lax.rem(band + i, 4) * 32, 32), 32), :] for i in range(4)]
    order = jnp.concatenate(order, axis=0)
    order_hi, order_lo = split(order)
    across_hi, across_lo = split(order.T)
    for i in range(4):
        part = slice(i * 32, i * 32 + 32)
        turned_rotation[i] = jnp.concatenate([across_hi[:, part], across_hi[:, part], across_lo[:, part]], axis=1)

    hand_on(0)

    for side in range(2):
        landed(exists[5 - side], lambda: z_copy(side))
    faces = []
    for quarter in range(4):
        block = pl.ds(quarter * 128, 128)
        faces.append(jnp.concatenate([z_land[0, :, block], z_land[1, :, block]], axis=1))
    faces_hi, faces_lo = split(jnp.concatenate(faces, axis=0))
    edge = dot(faces_hi, face_hi[...]) + dot(faces_lo, face_hi[...]) + dot(faces_hi, face_lo[...])
    for quarter in range(4):
        filt[:, pl.ds(quarter * QUARTER, QUARTER)] += edge[quarter * 32 : quarter * 32 + 32]

    loads[6].wait()
    lane = lax.broadcasted_iota(jnp.int32, (8, 128), 1) // 32
    mixing = []
    for j in range(8):
        column = jnp.zeros((8, 128), F32)
        for a in range(4):
            column = jnp.where(lane == a, coupling[a][:, j : j + 1], column)
        mixing.append(column)
    owned = messages[0]
    for direction in range(6):
        landed(exists[direction ^ 1], lambda: s_copy(direction))
        owned = owned + s_land[direction]
    coef = mixing[0] * owned[0:1, :]
    for j in range(1, 8):
        coef = coef + mixing[j] * owned[j : j + 1, :]
    c_send[...] = coef
    t_send[:, 0:128] = coef
    for direction in range(6):
        start(exists[direction], lambda: c_copy(direction))
    y_start(5)
    y_start(6)
    x_start(5)
    x_start(6)

    left_half = lax.broadcasted_iota(jnp.int32, (8, 128), 1) < 64

    def finish(k):
        quarter = quarter_of(k)
        for side in range(2):

            @pl.when(exists[side ^ 1] & x_used(side, k))
            def _():
                for m in (2 * k, 2 * k + 1):
                    x_copy(side, m)[0].wait_recv()
                block = pl.ds(lanes(quarter), QUARTER)
                filt[:, block] += x_land[side, :, block]

        y_landed(k)

        def line(n, _):
            rows = pl.ds(pl.multiple_of(lax.rem(n, 4) * 8, 8), 8)
            begin = lanes(quarter) + n // 4 * LINE

            def at(offset):
                return pl.ds(pl.multiple_of(begin + offset, 128), 128)

            run = [y_land[0, rows, at(128 + 128 * i)] for i in range(3)]
            run += [states[rows, at(128 * i)] for i in range(4)]
            run += [y_land[1, rows, at(128 * i)] for i in range(3)]
            turned = [pltpu.roll(v, 64, 1) for v in run]
            odd = []
            for g in range(3, 8):
                odd.append(
                    W[1] * (turned[g] + turned[g - 1])
                    + W[3] * (turned[min(g + 1, 9)] + turned[g - 2])
                    + W[5] * (turned[min(g + 2, 9)] + turned[g - 3])
                )
            for g in range(4):
                total = filt[rows, at(128 * g)]
                for n_far in (2, 4, 6):
                    total = total + W[n_far] * (run[g + 3 + n_far // 2] + run[g + 3 - n_far // 2])
                filt[rows, at(128 * g)] = total + jnp.where(left_half, odd[g], odd[g + 1])
            return 0

        lax.fori_loop(0, 8, line, 0, unroll=8)

    def rotated(value, i):
        high, low = split(value)
        return dot(turned_rotation[i], jnp.concatenate([high, low, high], axis=0))

    def arrived(k):
        landed(always, lambda: f_copy(k))
        total_t[...] += rotated(f_land[k], 3 - k)

    finish(0)
    start(always, lambda: f_copy(0))
    hand_on(1)

    for direction in range(6):
        landed(exists[direction ^ 1], lambda: c_copy(direction))
    for direction in range(6):
        t_send[:, pl.ds((direction + 1) * 128, 128)] = c_land[direction ^ 1]
    for i in range(3):
        start(always, lambda: t_copy(i))
    y_start(7)
    x_start(7)
    finish(1)
    start(always, lambda: f_copy(1))
    hand_on(2)

    finish(2)
    start(always, lambda: f_copy(2))

    tables = [t_send]
    for i in range(3):
        landed(always, lambda: t_copy(i))
    tables += [t_land.at[2 - i] for i in range(3)]
    known = []
    for group in range(28):
        known.append(jnp.concatenate([table[:, group * 32 : group * 32 + 32] for table in tables], axis=1))
    known_hi, known_lo = split(jnp.concatenate(known, axis=0))
    mixed = 0.15 * (dot(known_hi, order_hi) + dot(known_lo, order_hi) + dot(known_hi, order_lo))
    of_tile = dot(jnp.concatenate(split(mixed.T), axis=0), member[...]).astype(BF16)
    mine = pl.ds(lanes(band), QUARTER)
    nonlocal_t = dot(of_tile, g_hi[:, mine])
    total_t[...] = nonlocal_t[0:128] + nonlocal_t[128:256] + dot(of_tile[0:128], g_lo[:, mine])

    arrived(0)
    arrived(1)
    finish(3)
    arrived(2)
    out[...] = (total_t[...] + rotated(filt[:, mine], 0)).T

    for m in range(8):
        if m < 6:
            sent(inner, lambda: y_all(m))
            sent(outer, lambda: y_near(m))
            sent(outer, lambda: y_relay(m))
        else:
            sent(always, lambda: y_near(m))
            sent(inner, lambda: y_aside(m))
            sent(outer, lambda: y_back(m))
        for side in range(2):
            sent(exists[side] & x_used(side, m // 2), lambda: x_copy(side, m))
    for side in range(2):
        sent(exists[4 + side], lambda: z_copy(side))
    for direction in range(6):
        sent(exists[direction], lambda: s_copy(direction))
        sent(exists[direction], lambda: c_copy(direction))
    for k in range(3):
        sent(always, lambda: f_copy(k))
        sent(always, lambda: t_copy(k))


def body(states, previous, potential, tile_atom, tile_cells, tile_count, projectors, coupling, rotation):
    vmem = pl.BlockSpec(memory_space=pltpu.VMEM)
    dma = pltpu.SemaphoreType.DMA
    operands = (
        states,
        previous,
        potential.reshape(1, -1),
        tile_atom.reshape(1, -1),
        tile_cells,
        projectors,
        coupling,
        rotation,
    )
    return pl.pallas_call(
        kernel,
        out_shape=jax.ShapeDtypeStruct((QUARTER, 128), F32),
        in_specs=[pl.BlockSpec(memory_space=pltpu.SMEM)] + [pl.BlockSpec(memory_space=pltpu.HBM)] * 8,
        out_specs=vmem,
        scratch_shapes=[
            *(pltpu.VMEM(operand.shape, operand.dtype) for operand in operands),
            dma((8,)),
            pltpu.VMEM((256, QUARTER), BF16),
            pltpu.VMEM((256, QUARTER), BF16),
            pltpu.VMEM((32, 4096), F32),
            pltpu.VMEM((2, 32, 4096), F32),
            pltpu.VMEM((32, QUARTER), F32),
            pltpu.VMEM((2, 32, 4096), F32),
            pltpu.VMEM((2, 32, 4096), F32),
            pltpu.VMEM((2, 32, 512), F32),
            pltpu.VMEM((2, 32, 512), F32),
            pltpu.VMEM((6, 8, 128), F32),
            pltpu.VMEM((6, 8, 128), F32),
            pltpu.VMEM((8, 128), F32),
            pltpu.VMEM((6, 8, 128), F32),
            pltpu.VMEM((3, 32, QUARTER), F32),
            pltpu.VMEM((8, 896), F32),
            pltpu.VMEM((3, 8, 896), F32),
            pltpu.VMEM((4, 128, 96), BF16),
            pltpu.VMEM((128, QUARTER), F32),
            pltpu.VMEM((512, 4096), BF16),
            pltpu.VMEM((512, 4096), BF16),
            pltpu.VMEM((224, 512), BF16),
            dma((7, 8)),
            dma((7, 8)),
            dma((2, 8)),
            dma((2, 8)),
            dma((2,)),
            dma((2,)),
            dma((6,)),
            dma((6,)),
            dma((6,)),
            dma((6,)),
            dma((3,)),
            dma((3,)),
            dma((3,)),
            dma((3,)),
            pltpu.SemaphoreType.REGULAR((2,)),
        ],
        compiler_params=pltpu.CompilerParams(
            collective_id=0, has_side_effects=True, vmem_limit_bytes=64 * 1024 * 1024
        ),
        name="chebyshev_step",
    )(tile_count, *operands)


def solution(mesh):
    placed = (
        P("band", "dom"),
        P("band", "dom"),
        P("dom"),
        P("dom"),
        P("dom", None),
        P("dom"),
        P("dom", None, None),
        P("dom", None, None),
        P(),
    )
    return jax.shard_map(
        body, mesh=mesh, in_specs=placed, out_specs=P(("dom", "band"), None), check_vma=False
    )
```

```python
import jax
import jax.numpy as jnp
from jax import lax
from jax.experimental import pallas as pl
from jax.experimental.pallas import tpu as pltpu
from jax.sharding import PartitionSpec as P

MESH = pl.DeviceIdType.MESH
F32 = jnp.float32
BF16 = jnp.bfloat16

STENCIL = (
    -5369.0 / 1800.0,
    12.0 / 7.0,
    -15.0 / 56.0,
    10.0 / 189.0,
    -1.0 / 112.0,
    2.0 / 1925.0,
    -1.0 / 16632.0,
)
W = tuple(-0.075 * w for w in STENCIL)
QUARTER = 1024
LINE = 512


def split(value):
    high = value.astype(BF16)
    return high, (value - high.astype(F32)).astype(BF16)


def faces_of(rows, columns):
    row = lax.broadcasted_iota(jnp.int32, (rows, 1), 0)
    column = lax.broadcasted_iota(jnp.int32, (rows, columns), 1)
    side, line, i = row // 128, (row // 8 & 15) * 64, row & 7
    used = i < 6
    cell = jnp.where(used, line + jnp.where(side == 0, 58 + i, i), -1)
    pick = jnp.where(column == cell, 1.0, 0.0).astype(BF16)
    face = jnp.zeros((rows, columns), F32)
    for n in range(1, 7):
        z = jnp.where(side == 0, n - 6 + i, 64 + i - n)
        place = jnp.where(used & (z >= 0) & (z < 64), line + z, -1)
        face = jnp.where(column == place, W[n], face)
    return pick, *split(face)


def inside_of(size):
    row = lax.broadcasted_iota(jnp.int32, (size, size), 0)
    column = lax.broadcasted_iota(jnp.int32, (size, size), 1)
    gap = jnp.where(row // 64 == column // 64, jnp.abs(row - column), 0)
    weight = jnp.zeros((size, size), F32)
    for n in range(1, 7):
        weight = jnp.where(gap == n, W[n], weight)
    return split(weight)


def dot(a, b, ca=1, cb=0):
    return lax.dot_general(a, b, (((ca,), (cb,)), ((), ())), preferred_element_type=F32)


def kernel(
    count_ref,
    states_in,
    previous_in,
    potential_in,
    atom_in,
    cells_in,
    projectors_in,
    coupling_in,
    rotation_in,
    out,
    states,
    previous,
    potential,
    tile_atom,
    tile_cells,
    projectors,
    coupling,
    rotation,
    load_sem,
    face_hi,
    face_lo,
    filt,
    y_land,
    aside,
    x_send,
    x_land,
    z_send,
    z_land,
    s_send,
    s_land,
    c_send,
    c_land,
    f_land,
    t_send,
    t_land,
    turned_rotation,
    total_t,
    g_hi,
    g_lo,
    member,
    y_ss,
    y_rs,
    x_ss,
    x_rs,
    z_ss,
    z_rs,
    s_ss,
    s_rs,
    c_ss,
    c_rs,
    f_ss,
    f_rs,
    t_ss,
    t_rs,
    ready,
):
    band = lax.axis_index("band")
    dom = lax.axis_index("dom")
    gz = lax.rem(dom, 4)
    gy = lax.rem(dom // 4, 4)
    gx = dom // 16
    steps = (16, -16, 4, -4, 1, -1)
    exists = (gx < 7, gx > 0, gy < 3, gy > 0, gz < 3, gz > 0)

    loads = [
        pltpu.make_async_copy(source, target, load_sem.at[n])
        for n, (source, target) in enumerate(
            (
                (states_in, states),
                (cells_in, tile_cells),
                (projectors_in, projectors),
                (atom_in, tile_atom),
                (previous_in, previous),
                (potential_in, potential),
                (coupling_in, coupling),
                (rotation_in, rotation),
            )
        )
    ]
    for load in loads:
        load.start()

    always = band >= 0

    def there(direction):
        return (band, dom + steps[direction])

    def quarter_of(k):
        return (lax.rem(band + 2, 4), 3 - band, band + 1 - 2 * lax.rem(band, 2), band)[k]

    def lanes(quarter):
        return pl.multiple_of(quarter * QUARTER, QUARTER)

    def remote(source, target, sent, landed, device):
        return pltpu.make_async_remote_copy(
            src_ref=source,
            dst_ref=target,
            send_sem=sent,
            recv_sem=landed,
            device_id=device,
            device_id_type=MESH,
        )

    def start(needed, copies):
        @pl.when(needed)
        def _():
            for copy in copies():
                copy.start()

    def landed(needed, copies):
        @pl.when(needed)
        def _():
            for copy in copies():
                copy.wait_recv()

    def sent(needed, copies):
        @pl.when(needed)
        def _():
            for copy in copies():
                copy.wait_send()

    outer = (gy == 0) | (gy == 3)
    inner = jnp.logical_not(outer)
    even = lax.rem(gy, 2) == 0
    partner = (band, jnp.where(even, dom + 4, dom - 4))
    far = (band, jnp.where(gy < 2, dom + 8, dom - 8))
    partner_side = jnp.where(even, 1, 0)
    near_six = jnp.where(even, 128, 0)
    far_six = 128 - near_six

    later = (exists[0] & (gx != 3), exists[1] & (gx == 4))
    earlier = (exists[0] & (gx == 3), exists[1] & (gx != 4))
    barrier = pltpu.get_barrier_semaphore()
    for direction in range(6):

        @pl.when(later[direction] if direction < 2 else exists[direction])
        def _():
            pl.semaphore_signal(barrier, inc=1, device_id=there(direction), device_id_type=MESH)

    for other in range(1, 4):
        pl.semaphore_signal(
            barrier, inc=1, device_id=(lax.rem(band + other, 4), dom), device_id_type=MESH
        )
    pl.semaphore_signal(barrier, inc=1, device_id=far, device_id_type=MESH)
    partners = 4
    for direction in range(6):
        partners = partners + jnp.where(earlier[direction] if direction < 2 else exists[direction], 1, 0)
    pl.semaphore_wait(barrier, partners)
    for side in range(2):

        @pl.when(earlier[side])
        def _():
            pl.semaphore_signal(ready.at[1 - side], inc=1, device_id=there(side), device_id_type=MESH)

    def later_ready():
        for side in range(2):

            @pl.when(later[side])
            def _():
                pl.semaphore_wait(ready.at[side], 1)

    def half(m):
        return pl.ds(m % 2 * 16, 16)

    def y_all(m):
        block = pl.ds(lanes(quarter_of(m // 2)), QUARTER)
        return [
            remote(
                states_in.at[half(m), block],
                y_land.at[1 - partner_side, half(m), block],
                y_ss.at[0, m],
                y_rs.at[0, m],
                partner,
            )
        ]

    def y_six(m, source, source_start, target, target_start, six, number, device):
        copies = []
        for i in range(2):
            here = pl.ds(pl.multiple_of(source_start + i * LINE + six, 128), 384)
            over_there = pl.ds(pl.multiple_of(target_start + i * LINE + six, 128), 384)
            copies.append(
                remote(
                    source.at[half(m), here],
                    target.at[half(m), over_there],
                    y_ss.at[number + i, m],
                    y_rs.at[number + i, m],
                    device,
                )
            )
        return copies

    def y_near(m):
        begin = lanes(quarter_of(m // 2))
        return y_six(m, states_in, begin, y_land.at[1 - partner_side], begin, near_six, 1, partner)

    def y_relay(m):
        begin = lanes(quarter_of(m // 2))
        return y_six(m, y_land.at[partner_side], begin, y_land.at[1 - partner_side], begin, near_six, 3, far)

    def y_aside(m):
        return y_six(m, states_in, lanes(quarter_of(3)), aside, 0, far_six, 5, far)

    def y_back(m):
        return y_six(m, aside, 0, y_land.at[partner_side], lanes(quarter_of(3)), far_six, 3, partner)

    def y_start(m):
        if m < 6:
            start(inner, lambda: y_all(m))
            start(outer, lambda: y_near(m))
        else:
            start(always, lambda: y_near(m))

    def hand_on(k):
        for m in (2 * k, 2 * k + 1):
            if k < 3:
                landed(outer, lambda: y_all(m))
                start(outer, lambda: y_relay(m))
            else:
                landed(outer, lambda: y_aside(m))
                start(outer, lambda: y_back(m))

    def y_landed(k):
        for m in (2 * k, 2 * k + 1):
            if k < 3:
                landed(inner, lambda: y_near(m))
                landed(inner, lambda: y_relay(m))
            else:
                landed(always, lambda: y_near(m))
                landed(inner, lambda: y_back(m))

    def x_copy(side, m):
        block = pl.ds(lanes(quarter_of(m // 2)), QUARTER)
        return [
            remote(
                x_send.at[side, half(m), block],
                x_land.at[side, half(m), block],
                x_ss.at[side, m],
                x_rs.at[side, m],
                there(side),
            )
        ]

    def x_used(side, k):
        return quarter_of(k) < 3 if side == 0 else quarter_of(k) > 0

    def x_start(m, to=exists):
        for side in range(2):
            start(to[side] & x_used(side, m // 2), lambda: x_copy(side, m))

    def z_copy(side):
        return [remote(z_send.at[side], z_land.at[side], z_ss.at[side], z_rs.at[side], there(4 + side))]

    def s_copy(direction):
        return [
            remote(
                s_send.at[direction], s_land.at[direction], s_ss.at[direction], s_rs.at[direction], there(direction)
            )
        ]

    def c_copy(direction):
        return [remote(c_send, c_land.at[direction], c_ss.at[direction], c_rs.at[direction], there(direction))]

    def f_copy(k):
        return [
            remote(
                filt.at[:, pl.ds(lanes(quarter_of(k)), QUARTER)],
                f_land.at[k],
                f_ss.at[k],
                f_rs.at[k],
                (quarter_of(k), dom),
            )
        ]

    def t_copy(i):
        return [remote(t_send, t_land.at[i], t_ss.at[i], t_rs.at[i], (quarter_of(i), dom))]

    y_start(0)
    y_start(1)
    y_start(2)
    for m in (6, 7):
        start(inner, lambda: y_aside(m))

    def x_parts(g, _):
        rows = pl.ds(pl.multiple_of(g * 8, 8), 8)
        for column in range(4):
            layer = [states[rows, pl.ds(x * LINE + column * 128, 128)] for x in range(8)]
            for target in range(6):
                total = W[6] * layer[target + 2]
                for m in range(target + 3, 8):
                    total = total + W[target + 8 - m] * layer[m]
                x_send[0, rows, pl.ds(target * LINE + column * 128, 128)] = total
            for target in range(2, 8):
                total = W[6] * layer[target - 2]
                for m in range(target - 2):
                    total = total + W[m + 8 - target] * layer[m]
                x_send[1, rows, pl.ds(target * LINE + column * 128, 128)] = total
        return 0

    loads[0].wait()
    lax.fori_loop(0, 4, x_parts, 0)
    x_start(0, earlier)
    x_start(1, earlier)
    x_start(2, earlier)

    pick, *face = faces_of(256, QUARTER)
    face_hi[...], face_lo[...] = face
    pieces = []
    for quarter in range(4):
        pieces.extend(split(states[:, pl.ds(quarter * QUARTER, QUARTER)]))
    picked = dot(jnp.concatenate(pieces, axis=0), pick, 1, 1)
    for quarter in range(4):
        both = picked[quarter * 64 : quarter * 64 + 32] + picked[quarter * 64 + 32 : quarter * 64 + 64]
        z_send[0, :, pl.ds(quarter * 128, 128)] = both[:, 0:128]
        z_send[1, :, pl.ds(quarter * 128, 128)] = both[:, 128:256]

    for side in range(2):
        start(exists[4 + side], lambda: z_copy(side))

        @pl.when(jnp.logical_not(exists[5 - side]))
        def _():
            z_land[side] = jnp.zeros((32, 512), F32)

        @pl.when(jnp.logical_not(exists[3 - side]))
        def _():
            y_land[side] = jnp.zeros((32, 4096), F32)

    for direction in range(6):

        @pl.when(jnp.logical_not(exists[direction ^ 1]))
        def _():
            s_land[direction] = jnp.zeros((8, 128), F32)
            c_land[direction] = jnp.zeros((8, 128), F32)

    loads[1].wait()
    loads[2].wait()

    low_row = lax.broadcasted_iota(jnp.int32, (256, 128), 0).astype(F32).astype(BF16)
    high_row = (lax.broadcasted_iota(jnp.int32, (16, 128), 0) // 8).astype(F32).astype(BF16)
    high_rows = [high_row + jnp.asarray(2 * h, BF16) for h in range(8)]
    zero, one = jnp.asarray(0, BF16), jnp.asarray(1, BF16)

    def tile_pair(pair, _):
        spread = []
        for which in range(2):
            t = pair * 2 + which
            cells = tile_cells[pl.ds(t, 1), :]
            high = jnp.broadcast_to((cells >> 8).astype(F32), (16, 128)).astype(BF16)
            low = jnp.broadcast_to((cells & 255).astype(F32), (16, 128)).astype(BF16)
            low = jnp.concatenate([low] * 16, axis=0)
            w = projectors[t]
            w_hi = w.astype(BF16).astype(F32)
            w_lo = w - w_hi
            w_hi = jnp.concatenate([w_hi, w_hi], axis=0).astype(BF16)
            w_lo = jnp.concatenate([w_lo, w_lo], axis=0).astype(BF16)
            here = [high == row for row in high_rows]
            left = jnp.concatenate(
                [
                    jnp.concatenate([jnp.where(mask, w_hi, zero) for mask in here], axis=0),
                    jnp.concatenate([jnp.where(mask, w_lo, zero) for mask in here], axis=0),
                ],
                axis=1,
            )
            hot = jnp.where(low_row == low, one, zero)
            spread.append(dot(left, jnp.concatenate([hot, hot], axis=1), 1, 1))
        rows = pl.ds(pl.multiple_of(pair * 16, 16), 16)
        for h in range(16):
            both = jnp.concatenate([spread[0][h * 8 : h * 8 + 8], spread[1][h * 8 : h * 8 + 8]], axis=0)
            both_hi, both_lo = split(both)
            g_hi[rows, pl.ds(h * 256, 256)] = both_hi
            g_lo[rows, pl.ds(h * 256, 256)] = both_lo
        return 0

    lax.fori_loop(0, 16, tile_pair, 0, unroll=8)
    later_ready()
    x_start(0, later)
    x_start(1, later)
    x_start(2, later)
    lax.fori_loop(16, 32, tile_pair, 0, unroll=8)

    loads[3].wait()
    relative = (tile_atom[...] - dom * 4).astype(F32).astype(BF16)
    repeat = (
        lax.broadcasted_iota(jnp.int32, (64, 512), 0) == lax.broadcasted_iota(jnp.int32, (64, 512), 1) // 8
    )
    owner = dot(
        jnp.broadcast_to(relative.astype(F32), (16, 64)).astype(BF16), jnp.where(repeat, 1.0, 0.0).astype(BF16)
    )[0:1]
    slot = lax.broadcasted_iota(jnp.int32, (1, 512), 1)
    owner = jnp.where(slot // 8 < count_ref[0], owner, 1000.0)
    row = lax.broadcasted_iota(jnp.int32, (32, 512), 0)
    same_j = (row & 7) == (lax.broadcasted_iota(jnp.int32, (32, 512), 1) & 7)
    atom = (row // 8).astype(F32)
    for number, step in enumerate((0,) + steps):
        match = same_j & (atom + 4.0 * step == owner)
        member[pl.ds(number * 32, 32), :] = jnp.where(match, 1.0, 0.0).astype(BF16)

    st_hi, st_lo = split(states[...])
    partial_hi = dot(g_hi[...], jnp.concatenate([st_hi, st_lo], axis=0), 1, 1)
    partial_value = partial_hi[:, 0:32] + partial_hi[:, 32:64] + dot(g_lo[...], st_hi, 1, 1)
    part_hi, part_lo = split(partial_value)
    sums = dot(member[...], part_hi) + dot(member[...], part_lo)
    messages = []
    for number in range(7):
        messages.append(
            jnp.concatenate([sums[number * 32 + a * 8 : number * 32 + a * 8 + 8] for a in range(4)], axis=1)
        )
    for direction in range(6):
        s_send[direction] = messages[direction + 1]
    for direction in range(6):
        start(exists[direction], lambda: s_copy(direction))
    y_start(3)
    y_start(4)
    x_start(3)
    x_start(4)
    hand_on(3)

    def base(g, _):
        rows = pl.ds(pl.multiple_of(g * 8, 8), 8)
        for column in range(4):
            layer = [states[rows, pl.ds(x * LINE + column * 128, 128)] for x in range(8)]
            for x in range(8):
                block = pl.ds(x * LINE + column * 128, 128)
                total = layer[x] * (3.0 * W[0] - 1.2 + 0.15 * potential[:, block]) - 0.3 * previous[rows, block]
                for k in range(1, 7):
                    pair = [layer[m] for m in (x - k, x + k) if 0 <= m < 8]
                    if pair:
                        total = total + W[k] * (pair[0] + pair[1] if len(pair) == 2 else pair[0])
                filt[rows, block] = total
        return 0

    for n in (4, 5):
        loads[n].wait()
    lax.fori_loop(0, 4, base, 0)
    blocks = [states[:, pl.ds(i * 256, 256)] for i in range(16)]
    tall_hi, tall_lo = split(jnp.concatenate(blocks, axis=0))
    in_hi, in_lo = inside_of(256)
    inside = dot(tall_hi, in_hi) + dot(tall_lo, in_hi) + dot(tall_hi, in_lo)
    for i in range(16):
        filt[:, pl.ds(i * 256, 256)] += inside[i * 32 : i * 32 + 32]

    loads[7].wait()
    order = [rotation[pl.ds(pl.multiple_of(source * 32, 32), 32), :] for source in (band, *map(quarter_of, range(3)))]
    order = jnp.concatenate(order, axis=0)
    order_hi, order_lo = split(order)
    across_hi, across_lo = split(order.T)
    for i in range(4):
        part = slice(i * 32, i * 32 + 32)
        turned_rotation[i] = jnp.concatenate([across_hi[:, part], across_hi[:, part], across_lo[:, part]], axis=1)

    hand_on(0)

    for side in range(2):
        landed(exists[5 - side], lambda: z_copy(side))
    faces = []
    for quarter in range(4):
        block = pl.ds(quarter * 128, 128)
        faces.append(jnp.concatenate([z_land[0, :, block], z_land[1, :, block]], axis=1))
    faces_hi, faces_lo = split(jnp.concatenate(faces, axis=0))
    edge = dot(faces_hi, face_hi[...]) + dot(faces_lo, face_hi[...]) + dot(faces_hi, face_lo[...])
    for quarter in range(4):
        filt[:, pl.ds(quarter * QUARTER, QUARTER)] += edge[quarter * 32 : quarter * 32 + 32]

    loads[6].wait()
    lane = lax.broadcasted_iota(jnp.int32, (8, 128), 1) // 32
    mixing = []
    for j in range(8):
        column = jnp.zeros((8, 128), F32)
        for a in range(4):
            column = jnp.where(lane == a, coupling[a][:, j : j + 1], column)
        mixing.append(column)
    owned = messages[0]
    for direction in range(6):
        landed(exists[direction ^ 1], lambda: s_copy(direction))
        owned = owned + s_land[direction]
    coef = mixing[0] * owned[0:1, :]
    for j in range(1, 8):
        coef = coef + mixing[j] * owned[j : j + 1, :]
    c_send[...] = coef
    t_send[:, 0:128] = coef
    for direction in range(6):
        start(exists[direction], lambda: c_copy(direction))
    y_start(5)
    y_start(6)
    x_start(5)
    x_start(6)

    left_half = lax.broadcasted_iota(jnp.int32, (8, 128), 1) < 64

    def finish(k):
        quarter = quarter_of(k)
        for side in range(2):

            @pl.when(exists[side ^ 1] & x_used(side, k))
            def _():
                for m in (2 * k, 2 * k + 1):
                    x_copy(side, m)[0].wait_recv()
                block = pl.ds(lanes(quarter), QUARTER)
                filt[:, block] += x_land[side, :, block]

        y_landed(k)

        def line(n, _):
            rows = pl.ds(pl.multiple_of(lax.rem(n, 4) * 8, 8), 8)
            begin = lanes(quarter) + n // 4 * LINE

            def at(offset):
                return pl.ds(pl.multiple_of(begin + offset, 128), 128)

            run = [y_land[0, rows, at(128 + 128 * i)] for i in range(3)]
            run += [states[rows, at(128 * i)] for i in range(4)]
            run += [y_land[1, rows, at(128 * i)] for i in range(3)]
            turned = [pltpu.roll(v, 64, 1) for v in run]
            odd = []
            for g in range(3, 8):
                odd.append(
                    W[1] * (turned[g] + turned[g - 1])
                    + W[3] * (turned[min(g + 1, 9)] + turned[g - 2])
                    + W[5] * (turned[min(g + 2, 9)] + turned[g - 3])
                )
            for g in range(4):
                total = filt[rows, at(128 * g)]
                for n_far in (2, 4, 6):
                    total = total + W[n_far] * (run[g + 3 + n_far // 2] + run[g + 3 - n_far // 2])
                filt[rows, at(128 * g)] = total + jnp.where(left_half, odd[g], odd[g + 1])
            return 0

        lax.fori_loop(0, 8, line, 0, unroll=8)

    def rotated(value, i):
        high, low = split(value)
        return dot(turned_rotation[i], jnp.concatenate([high, low, high], axis=0))

    def arrived(k):
        landed(always, lambda: f_copy(k))
        total_t[...] += rotated(f_land[k], k + 1)

    finish(0)
    start(always, lambda: f_copy(0))
    hand_on(1)

    for direction in range(6):
        landed(exists[direction ^ 1], lambda: c_copy(direction))
    for direction in range(6):
        t_send[:, pl.ds((direction + 1) * 128, 128)] = c_land[direction ^ 1]
    for i in range(3):
        start(always, lambda: t_copy(i))
    y_start(7)
    x_start(7)
    hand_on(2)
    finish(1)
    start(always, lambda: f_copy(1))

    finish(2)
    start(always, lambda: f_copy(2))

    tables = [t_send]
    for i in range(3):
        landed(always, lambda: t_copy(i))
    tables += [t_land.at[i] for i in range(3)]
    known = []
    for group in range(28):
        known.append(jnp.concatenate([table[:, group * 32 : group * 32 + 32] for table in tables], axis=1))
    known_hi, known_lo = split(jnp.concatenate(known, axis=0))
    mixed = 0.15 * (dot(known_hi, order_hi) + dot(known_lo, order_hi) + dot(known_hi, order_lo))
    of_tile = dot(jnp.concatenate(split(mixed.T), axis=0), member[...]).astype(BF16)
    mine = pl.ds(lanes(band), QUARTER)
    nonlocal_t = dot(of_tile, g_hi[:, mine])
    total_t[...] = nonlocal_t[0:128] + nonlocal_t[128:256] + dot(of_tile[0:128], g_lo[:, mine])

    arrived(0)
    arrived(1)
    finish(3)
    arrived(2)
    out[...] = (total_t[...] + rotated(filt[:, mine], 0)).T

    for m in range(8):
        if m < 6:
            sent(inner, lambda: y_all(m))
            sent(outer, lambda: y_near(m))
            sent(outer, lambda: y_relay(m))
        else:
            sent(always, lambda: y_near(m))
            sent(inner, lambda: y_aside(m))
            sent(outer, lambda: y_back(m))
        for side in range(2):
            sent(exists[side] & x_used(side, m // 2), lambda: x_copy(side, m))
    for side in range(2):
        sent(exists[4 + side], lambda: z_copy(side))
    for direction in range(6):
        sent(exists[direction], lambda: s_copy(direction))
        sent(exists[direction], lambda: c_copy(direction))
    for k in range(3):
        sent(always, lambda: f_copy(k))
        sent(always, lambda: t_copy(k))


def body(states, previous, potential, tile_atom, tile_cells, tile_count, projectors, coupling, rotation):
    vmem = pl.BlockSpec(memory_space=pltpu.VMEM)
    dma = pltpu.SemaphoreType.DMA
    operands = (
        states,
        previous,
        potential.reshape(1, -1),
        tile_atom.reshape(1, -1),
        tile_cells,
        projectors,
        coupling,
        rotation,
    )
    return pl.pallas_call(
        kernel,
        out_shape=jax.ShapeDtypeStruct((QUARTER, 128), F32),
        in_specs=[pl.BlockSpec(memory_space=pltpu.SMEM)] + [pl.BlockSpec(memory_space=pltpu.HBM)] * 8,
        out_specs=vmem,
        scratch_shapes=[
            *(pltpu.VMEM(operand.shape, operand.dtype) for operand in operands),
            dma((8,)),
            pltpu.VMEM((256, QUARTER), BF16),
            pltpu.VMEM((256, QUARTER), BF16),
            pltpu.VMEM((32, 4096), F32),
            pltpu.VMEM((2, 32, 4096), F32),
            pltpu.VMEM((32, QUARTER), F32),
            pltpu.VMEM((2, 32, 4096), F32),
            pltpu.VMEM((2, 32, 4096), F32),
            pltpu.VMEM((2, 32, 512), F32),
            pltpu.VMEM((2, 32, 512), F32),
            pltpu.VMEM((6, 8, 128), F32),
            pltpu.VMEM((6, 8, 128), F32),
            pltpu.VMEM((8, 128), F32),
            pltpu.VMEM((6, 8, 128), F32),
            pltpu.VMEM((3, 32, QUARTER), F32),
            pltpu.VMEM((8, 896), F32),
            pltpu.VMEM((3, 8, 896), F32),
            pltpu.VMEM((4, 128, 96), BF16),
            pltpu.VMEM((128, QUARTER), F32),
            pltpu.VMEM((512, 4096), BF16),
            pltpu.VMEM((512, 4096), BF16),
            pltpu.VMEM((224, 512), BF16),
            dma((7, 8)),
            dma((7, 8)),
            dma((2, 8)),
            dma((2, 8)),
            dma((2,)),
            dma((2,)),
            dma((6,)),
            dma((6,)),
            dma((6,)),
            dma((6,)),
            dma((3,)),
            dma((3,)),
            dma((3,)),
            dma((3,)),
            pltpu.SemaphoreType.REGULAR((2,)),
        ],
        compiler_params=pltpu.CompilerParams(
            collective_id=0, has_side_effects=True, vmem_limit_bytes=64 * 1024 * 1024
        ),
        name="chebyshev_step",
    )(tile_count, *operands)


def solution(mesh):
    placed = (
        P("band", "dom"),
        P("band", "dom"),
        P("dom"),
        P("dom"),
        P("dom", None),
        P("dom"),
        P("dom", None, None),
        P("dom", None, None),
        P(),
    )
    return jax.shard_map(
        body, mesh=mesh, in_specs=placed, out_specs=P(("dom", "band"), None), check_vma=False
    )
```

```python
import jax
import jax.numpy as jnp
from jax import lax
from jax.experimental import pallas as pl
from jax.experimental.pallas import tpu as pltpu
from jax.sharding import PartitionSpec as P

MESH = pl.DeviceIdType.MESH
F32 = jnp.float32
BF16 = jnp.bfloat16

STENCIL = (
    -5369.0 / 1800.0,
    12.0 / 7.0,
    -15.0 / 56.0,
    10.0 / 189.0,
    -1.0 / 112.0,
    2.0 / 1925.0,
    -1.0 / 16632.0,
)
W = tuple(-0.075 * w for w in STENCIL)
QUARTER = 1024
LINE = 512


def split(value):
    high = value.astype(BF16)
    return high, (value - high.astype(F32)).astype(BF16)


def faces_of(rows, columns):
    row = lax.broadcasted_iota(jnp.int32, (rows, 1), 0)
    column = lax.broadcasted_iota(jnp.int32, (rows, columns), 1)
    side, line, i = row // 128, (row // 8 & 15) * 64, row & 7
    used = i < 6
    cell = jnp.where(used, line + jnp.where(side == 0, 58 + i, i), -1)
    pick = jnp.where(column == cell, 1.0, 0.0).astype(BF16)
    face = jnp.zeros((rows, columns), F32)
    for n in range(1, 7):
        z = jnp.where(side == 0, n - 6 + i, 64 + i - n)
        place = jnp.where(used & (z >= 0) & (z < 64), line + z, -1)
        face = jnp.where(column == place, W[n], face)
    return pick, *split(face)


def inside_of(size):
    row = lax.broadcasted_iota(jnp.int32, (size, size), 0)
    column = lax.broadcasted_iota(jnp.int32, (size, size), 1)
    gap = jnp.where(row // 64 == column // 64, jnp.abs(row - column), 0)
    weight = jnp.zeros((size, size), F32)
    for n in range(1, 7):
        weight = jnp.where(gap == n, W[n], weight)
    return split(weight)


def dot(a, b, ca=1, cb=0):
    return lax.dot_general(a, b, (((ca,), (cb,)), ((), ())), preferred_element_type=F32)


def kernel(
    count_ref,
    states_in,
    previous_in,
    potential_in,
    atom_in,
    cells_in,
    projectors_in,
    coupling_in,
    rotation_in,
    out,
    states,
    previous,
    potential,
    tile_atom,
    tile_cells,
    projectors,
    coupling,
    rotation,
    load_sem,
    face_hi,
    face_lo,
    filt,
    y_land,
    aside,
    x_send,
    x_land,
    z_send,
    z_land,
    s_send,
    s_land,
    c_send,
    c_land,
    f_land,
    t_send,
    t_land,
    turned_rotation,
    total_t,
    g_hi,
    g_lo,
    member,
    y_ss,
    y_rs,
    x_ss,
    x_rs,
    z_ss,
    z_rs,
    s_ss,
    s_rs,
    c_ss,
    c_rs,
    f_ss,
    f_rs,
    t_ss,
    t_rs,
    ready,
):
    band = lax.axis_index("band")
    dom = lax.axis_index("dom")
    gz = lax.rem(dom, 4)
    gy = lax.rem(dom // 4, 4)
    gx = dom // 16
    steps = (16, -16, 4, -4, 1, -1)
    exists = (gx < 7, gx > 0, gy < 3, gy > 0, gz < 3, gz > 0)

    loads = [
        pltpu.make_async_copy(source, target, load_sem.at[n])
        for n, (source, target) in enumerate(
            (
                (states_in, states),
                (cells_in, tile_cells),
                (projectors_in, projectors),
                (atom_in, tile_atom),
                (previous_in, previous),
                (potential_in, potential),
                (coupling_in, coupling),
                (rotation_in, rotation),
            )
        )
    ]
    for load in loads:
        load.start()

    always = band >= 0

    def there(direction):
        return (band, dom + steps[direction])

    def quarter_of(k):
        return (lax.rem(band + 2, 4), 3 - band, band + 1 - 2 * lax.rem(band, 2), band)[k]

    def lanes(quarter):
        return pl.multiple_of(quarter * QUARTER, QUARTER)

    def remote(source, target, sent, landed, device):
        return pltpu.make_async_remote_copy(
            src_ref=source,
            dst_ref=target,
            send_sem=sent,
            recv_sem=landed,
            device_id=device,
            device_id_type=MESH,
        )

    def start(needed, copies):
        @pl.when(needed)
        def _():
            for copy in copies():
                copy.start()

    def landed(needed, copies):
        @pl.when(needed)
        def _():
            for copy in copies():
                copy.wait_recv()

    def sent(needed, copies):
        @pl.when(needed)
        def _():
            for copy in copies():
                copy.wait_send()

    outer = (gy == 0) | (gy == 3)
    inner = jnp.logical_not(outer)
    even = lax.rem(gy, 2) == 0
    partner = (band, jnp.where(even, dom + 4, dom - 4))
    far = (band, jnp.where(gy < 2, dom + 8, dom - 8))
    partner_side = jnp.where(even, 1, 0)
    near_six = jnp.where(even, 128, 0)
    far_six = 128 - near_six

    later = (exists[0] & (gx != 3), exists[1] & (gx == 4))
    earlier = (exists[0] & (gx == 3), exists[1] & (gx != 4))
    barrier = pltpu.get_barrier_semaphore()
    for direction in range(6):

        @pl.when(later[direction] if direction < 2 else exists[direction])
        def _():
            pl.semaphore_signal(barrier, inc=1, device_id=there(direction), device_id_type=MESH)

    for other in range(1, 4):
        pl.semaphore_signal(
            barrier, inc=1, device_id=(lax.rem(band + other, 4), dom), device_id_type=MESH
        )
    pl.semaphore_signal(barrier, inc=1, device_id=far, device_id_type=MESH)
    partners = 4
    for direction in range(6):
        partners = partners + jnp.where(earlier[direction] if direction < 2 else exists[direction], 1, 0)
    pl.semaphore_wait(barrier, partners)
    for side in range(2):

        @pl.when(earlier[side])
        def _():
            pl.semaphore_signal(ready.at[1 - side], inc=1, device_id=there(side), device_id_type=MESH)

    def later_ready():
        for side in range(2):

            @pl.when(later[side])
            def _():
                pl.semaphore_wait(ready.at[side], 1)

    def half(m):
        return pl.ds(m % 2 * 16, 16)

    def y_all(m):
        block = pl.ds(lanes(quarter_of(m // 2)), QUARTER)
        return [
            remote(
                states_in.at[half(m), block],
                y_land.at[1 - partner_side, half(m), block],
                y_ss.at[0, m],
                y_rs.at[0, m],
                partner,
            )
        ]

    def y_six(m, source, source_start, target, target_start, six, number, device):
        copies = []
        for i in range(2):
            here = pl.ds(pl.multiple_of(source_start + i * LINE + six, 128), 384)
            over_there = pl.ds(pl.multiple_of(target_start + i * LINE + six, 128), 384)
            copies.append(
                remote(
                    source.at[half(m), here],
                    target.at[half(m), over_there],
                    y_ss.at[number + i, m],
                    y_rs.at[number + i, m],
                    device,
                )
            )
        return copies

    def y_near(m):
        begin = lanes(quarter_of(m // 2))
        return y_six(m, states_in, begin, y_land.at[1 - partner_side], begin, near_six, 1, partner)

    def y_relay(m):
        begin = lanes(quarter_of(m // 2))
        return y_six(m, y_land.at[partner_side], begin, y_land.at[1 - partner_side], begin, near_six, 3, far)

    def y_aside(m):
        return y_six(m, states_in, lanes(quarter_of(3)), aside, 0, far_six, 5, far)

    def y_back(m):
        return y_six(m, aside, 0, y_land.at[partner_side], lanes(quarter_of(3)), far_six, 3, partner)

    def y_start(m):
        if m < 6:
            start(inner, lambda: y_all(m))
            start(outer, lambda: y_near(m))
        else:
            start(always, lambda: y_near(m))

    def hand_on(k):
        for m in (2 * k, 2 * k + 1):
            if k < 3:
                landed(outer, lambda: y_all(m))
                start(outer, lambda: y_relay(m))
            else:
                landed(outer, lambda: y_aside(m))
                start(outer, lambda: y_back(m))

    def y_landed(k):
        for m in (2 * k, 2 * k + 1):
            if k < 3:
                landed(inner, lambda: y_near(m))
                landed(inner, lambda: y_relay(m))
            else:
                landed(always, lambda: y_near(m))
                landed(inner, lambda: y_back(m))

    def x_copy(side, m):
        block = pl.ds(lanes(quarter_of(m // 2)), QUARTER)
        return [
            remote(
                x_send.at[side, half(m), block],
                x_land.at[side, half(m), block],
                x_ss.at[side, m],
                x_rs.at[side, m],
                there(side),
            )
        ]

    def x_used(side, k):
        return quarter_of(k) < 3 if side == 0 else quarter_of(k) > 0

    def x_start(m, to=exists):
        for side in range(2):
            start(to[side] & x_used(side, m // 2), lambda: x_copy(side, m))

    def z_copy(side):
        return [remote(z_send.at[side], z_land.at[side], z_ss.at[side], z_rs.at[side], there(4 + side))]

    def s_copy(direction):
        return [
            remote(
                s_send.at[direction], s_land.at[direction], s_ss.at[direction], s_rs.at[direction], there(direction)
            )
        ]

    def c_copy(direction):
        return [remote(c_send, c_land.at[direction], c_ss.at[direction], c_rs.at[direction], there(direction))]

    def f_copy(k):
        return [
            remote(
                filt.at[:, pl.ds(lanes(quarter_of(k)), QUARTER)],
                f_land.at[k],
                f_ss.at[k],
                f_rs.at[k],
                (quarter_of(k), dom),
            )
        ]

    def t_copy(i):
        return [remote(t_send, t_land.at[i], t_ss.at[i], t_rs.at[i], (quarter_of(i), dom))]

    y_start(0)
    y_start(1)
    y_start(2)
    for m in (6, 7):
        start(inner, lambda: y_aside(m))

    def x_parts(g, _):
        rows = pl.ds(pl.multiple_of(g * 8, 8), 8)
        for column in range(4):
            layer = [states[rows, pl.ds(x * LINE + column * 128, 128)] for x in range(8)]
            for target in range(6):
                total = W[6] * layer[target + 2]
                for m in range(target + 3, 8):
                    total = total + W[target + 8 - m] * layer[m]
                x_send[0, rows, pl.ds(target * LINE + column * 128, 128)] = total
            for target in range(2, 8):
                total = W[6] * layer[target - 2]
                for m in range(target - 2):
                    total = total + W[m + 8 - target] * layer[m]
                x_send[1, rows, pl.ds(target * LINE + column * 128, 128)] = total
        return 0

    loads[0].wait()
    lax.fori_loop(0, 4, x_parts, 0)
    x_start(0, earlier)
    x_start(1, earlier)
    x_start(2, earlier)

    pick, *face = faces_of(256, QUARTER)
    face_hi[...], face_lo[...] = face
    pieces = []
    for quarter in range(4):
        pieces.extend(split(states[:, pl.ds(quarter * QUARTER, QUARTER)]))
    picked = dot(jnp.concatenate(pieces, axis=0), pick, 1, 1)
    for quarter in range(4):
        both = picked[quarter * 64 : quarter * 64 + 32] + picked[quarter * 64 + 32 : quarter * 64 + 64]
        z_send[0, :, pl.ds(quarter * 128, 128)] = both[:, 0:128]
        z_send[1, :, pl.ds(quarter * 128, 128)] = both[:, 128:256]

    for side in range(2):
        start(exists[4 + side], lambda: z_copy(side))

        @pl.when(jnp.logical_not(exists[5 - side]))
        def _():
            z_land[side] = jnp.zeros((32, 512), F32)

        @pl.when(jnp.logical_not(exists[3 - side]))
        def _():
            y_land[side] = jnp.zeros((32, 4096), F32)

    for direction in range(6):

        @pl.when(jnp.logical_not(exists[direction ^ 1]))
        def _():
            s_land[direction] = jnp.zeros((8, 128), F32)
            c_land[direction] = jnp.zeros((8, 128), F32)

    loads[1].wait()
    loads[2].wait()

    low_row = lax.broadcasted_iota(jnp.int32, (256, 128), 0).astype(F32).astype(BF16)
    high_row = (lax.broadcasted_iota(jnp.int32, (16, 128), 0) // 8).astype(F32).astype(BF16)
    high_rows = [high_row + jnp.asarray(2 * h, BF16) for h in range(8)]
    zero, one = jnp.asarray(0, BF16), jnp.asarray(1, BF16)

    def tile_pair(pair, _):
        spread = []
        for which in range(2):
            t = pair * 2 + which
            cells = tile_cells[pl.ds(t, 1), :]
            high = jnp.broadcast_to((cells >> 8).astype(F32), (16, 128)).astype(BF16)
            low = jnp.broadcast_to((cells & 255).astype(F32), (16, 128)).astype(BF16)
            low = jnp.concatenate([low] * 16, axis=0)
            w = projectors[t]
            w_hi = w.astype(BF16).astype(F32)
            w_lo = w - w_hi
            w_hi = jnp.concatenate([w_hi, w_hi], axis=0).astype(BF16)
            w_lo = jnp.concatenate([w_lo, w_lo], axis=0).astype(BF16)
            here = [high == row for row in high_rows]
            left = jnp.concatenate(
                [
                    jnp.concatenate([jnp.where(mask, w_hi, zero) for mask in here], axis=0),
                    jnp.concatenate([jnp.where(mask, w_lo, zero) for mask in here], axis=0),
                ],
                axis=1,
            )
            hot = jnp.where(low_row == low, one, zero)
            spread.append(dot(left, jnp.concatenate([hot, hot], axis=1), 1, 1))
        rows = pl.ds(pl.multiple_of(pair * 16, 16), 16)
        for h in range(16):
            both = jnp.concatenate([spread[0][h * 8 : h * 8 + 8], spread[1][h * 8 : h * 8 + 8]], axis=0)
            both_hi, both_lo = split(both)
            g_hi[rows, pl.ds(h * 256, 256)] = both_hi
            g_lo[rows, pl.ds(h * 256, 256)] = both_lo
        return 0

    lax.fori_loop(0, 16, tile_pair, 0, unroll=8)
    later_ready()
    x_start(0, later)
    x_start(1, later)
    x_start(2, later)
    lax.fori_loop(16, 32, tile_pair, 0, unroll=8)

    loads[3].wait()
    relative = (tile_atom[...] - dom * 4).astype(F32).astype(BF16)
    repeat = (
        lax.broadcasted_iota(jnp.int32, (64, 512), 0) == lax.broadcasted_iota(jnp.int32, (64, 512), 1) // 8
    )
    owner = dot(
        jnp.broadcast_to(relative.astype(F32), (16, 64)).astype(BF16), jnp.where(repeat, 1.0, 0.0).astype(BF16)
    )[0:1]
    slot = lax.broadcasted_iota(jnp.int32, (1, 512), 1)
    owner = jnp.where(slot // 8 < count_ref[0], owner, 1000.0)
    row = lax.broadcasted_iota(jnp.int32, (32, 512), 0)
    same_j = (row & 7) == (lax.broadcasted_iota(jnp.int32, (32, 512), 1) & 7)
    atom = (row // 8).astype(F32)
    for number, step in enumerate((0,) + steps):
        match = same_j & (atom + 4.0 * step == owner)
        member[pl.ds(number * 32, 32), :] = jnp.where(match, 1.0, 0.0).astype(BF16)

    st_hi, st_lo = split(states[...])
    partial_hi = dot(g_hi[...], jnp.concatenate([st_hi, st_lo], axis=0), 1, 1)
    partial_value = partial_hi[:, 0:32] + partial_hi[:, 32:64] + dot(g_lo[...], st_hi, 1, 1)
    part_hi, part_lo = split(partial_value)
    sums = dot(member[...], part_hi) + dot(member[...], part_lo)
    messages = []
    for number in range(7):
        messages.append(
            jnp.concatenate([sums[number * 32 + a * 8 : number * 32 + a * 8 + 8] for a in range(4)], axis=1)
        )
    for direction in range(6):
        s_send[direction] = messages[direction + 1]
    for direction in range(6):
        start(exists[direction], lambda: s_copy(direction))
    y_start(3)
    y_start(4)
    x_start(3)
    x_start(4)
    hand_on(3)

    def base(g, _):
        rows = pl.ds(pl.multiple_of(g * 8, 8), 8)
        for column in range(4):
            layer = [states[rows, pl.ds(x * LINE + column * 128, 128)] for x in range(8)]
            for x in range(8):
                block = pl.ds(x * LINE + column * 128, 128)
                total = layer[x] * (3.0 * W[0] - 1.2 + 0.15 * potential[:, block]) - 0.3 * previous[rows, block]
                for k in range(1, 7):
                    pair = [layer[m] for m in (x - k, x + k) if 0 <= m < 8]
                    if pair:
                        total = total + W[k] * (pair[0] + pair[1] if len(pair) == 2 else pair[0])
                filt[rows, block] = total
        return 0

    for n in (4, 5):
        loads[n].wait()
    lax.fori_loop(0, 4, base, 0)
    blocks = [states[:, pl.ds(i * 256, 256)] for i in range(16)]
    tall_hi, tall_lo = split(jnp.concatenate(blocks, axis=0))
    in_hi, in_lo = inside_of(256)
    inside = dot(tall_hi, in_hi) + dot(tall_lo, in_hi) + dot(tall_hi, in_lo)
    for i in range(16):
        filt[:, pl.ds(i * 256, 256)] += inside[i * 32 : i * 32 + 32]

    loads[7].wait()
    order = [rotation[pl.ds(pl.multiple_of(source * 32, 32), 32), :] for source in (band, *map(quarter_of, range(3)))]
    order = jnp.concatenate(order, axis=0)
    order_hi, order_lo = split(order)
    across_hi, across_lo = split(order.T)
    for i in range(4):
        part = slice(i * 32, i * 32 + 32)
        turned_rotation[i] = jnp.concatenate([across_hi[:, part], across_hi[:, part], across_lo[:, part]], axis=1)

    hand_on(0)

    for side in range(2):
        landed(exists[5 - side], lambda: z_copy(side))
    faces = []
    for quarter in range(4):
        block = pl.ds(quarter * 128, 128)
        faces.append(jnp.concatenate([z_land[0, :, block], z_land[1, :, block]], axis=1))
    faces_hi, faces_lo = split(jnp.concatenate(faces, axis=0))
    edge = dot(faces_hi, face_hi[...]) + dot(faces_lo, face_hi[...]) + dot(faces_hi, face_lo[...])
    for quarter in range(4):
        filt[:, pl.ds(quarter * QUARTER, QUARTER)] += edge[quarter * 32 : quarter * 32 + 32]

    loads[6].wait()
    lane = lax.broadcasted_iota(jnp.int32, (8, 128), 1) // 32
    mixing = []
    for j in range(8):
        column = jnp.zeros((8, 128), F32)
        for a in range(4):
            column = jnp.where(lane == a, coupling[a][:, j : j + 1], column)
        mixing.append(column)
    owned = messages[0]
    for direction in range(6):
        landed(exists[direction ^ 1], lambda: s_copy(direction))
        owned = owned + s_land[direction]
    coef = mixing[0] * owned[0:1, :]
    for j in range(1, 8):
        coef = coef + mixing[j] * owned[j : j + 1, :]
    c_send[...] = coef
    t_send[:, 0:128] = coef
    for direction in range(6):
        start(exists[direction], lambda: c_copy(direction))
    y_start(5)
    y_start(6)
    y_start(7)
    x_start(5)
    x_start(6)

    left_half = lax.broadcasted_iota(jnp.int32, (8, 128), 1) < 64

    def finish(k):
        quarter = quarter_of(k)
        for side in range(2):

            @pl.when(exists[side ^ 1] & x_used(side, k))
            def _():
                for m in (2 * k, 2 * k + 1):
                    x_copy(side, m)[0].wait_recv()
                block = pl.ds(lanes(quarter), QUARTER)
                filt[:, block] += x_land[side, :, block]

        y_landed(k)

        def line(n, _):
            rows = pl.ds(pl.multiple_of(lax.rem(n, 4) * 8, 8), 8)
            begin = lanes(quarter) + n // 4 * LINE

            def at(offset):
                return pl.ds(pl.multiple_of(begin + offset, 128), 128)

            run = [y_land[0, rows, at(128 + 128 * i)] for i in range(3)]
            run += [states[rows, at(128 * i)] for i in range(4)]
            run += [y_land[1, rows, at(128 * i)] for i in range(3)]
            turned = [pltpu.roll(v, 64, 1) for v in run]
            odd = []
            for g in range(3, 8):
                odd.append(
                    W[1] * (turned[g] + turned[g - 1])
                    + W[3] * (turned[min(g + 1, 9)] + turned[g - 2])
                    + W[5] * (turned[min(g + 2, 9)] + turned[g - 3])
                )
            for g in range(4):
                total = filt[rows, at(128 * g)]
                for n_far in (2, 4, 6):
                    total = total + W[n_far] * (run[g + 3 + n_far // 2] + run[g + 3 - n_far // 2])
                filt[rows, at(128 * g)] = total + jnp.where(left_half, odd[g], odd[g + 1])
            return 0

        lax.fori_loop(0, 8, line, 0, unroll=8)

    def rotated(value, i):
        high, low = split(value)
        return dot(turned_rotation[i], jnp.concatenate([high, low, high], axis=0))

    def arrived(k):
        landed(always, lambda: f_copy(k))
        total_t[...] += rotated(f_land[k], k + 1)

    finish(0)
    start(always, lambda: f_copy(0))
    hand_on(1)

    for direction in range(6):
        landed(exists[direction ^ 1], lambda: c_copy(direction))
    for direction in range(6):
        t_send[:, pl.ds((direction + 1) * 128, 128)] = c_land[direction ^ 1]
    for i in range(3):
        start(always, lambda: t_copy(i))
    x_start(7)
    hand_on(2)
    finish(1)
    start(always, lambda: f_copy(1))

    finish(2)
    start(always, lambda: f_copy(2))

    tables = [t_send]
    for i in range(3):
        landed(always, lambda: t_copy(i))
    tables += [t_land.at[i] for i in range(3)]
    known = []
    for group in range(28):
        known.append(jnp.concatenate([table[:, group * 32 : group * 32 + 32] for table in tables], axis=1))
    known_hi, known_lo = split(jnp.concatenate(known, axis=0))
    mixed = 0.15 * (dot(known_hi, order_hi) + dot(known_lo, order_hi) + dot(known_hi, order_lo))
    of_tile = dot(jnp.concatenate(split(mixed.T), axis=0), member[...]).astype(BF16)
    mine = pl.ds(lanes(band), QUARTER)
    nonlocal_t = dot(of_tile, g_hi[:, mine])
    total_t[...] = nonlocal_t[0:128] + nonlocal_t[128:256] + dot(of_tile[0:128], g_lo[:, mine])

    arrived(0)
    arrived(1)
    finish(3)
    arrived(2)
    out[...] = (total_t[...] + rotated(filt[:, mine], 0)).T

    for m in range(8):
        if m < 6:
            sent(inner, lambda: y_all(m))
            sent(outer, lambda: y_near(m))
            sent(outer, lambda: y_relay(m))
        else:
            sent(always, lambda: y_near(m))
            sent(inner, lambda: y_aside(m))
            sent(outer, lambda: y_back(m))
        for side in range(2):
            sent(exists[side] & x_used(side, m // 2), lambda: x_copy(side, m))
    for side in range(2):
        sent(exists[4 + side], lambda: z_copy(side))
    for direction in range(6):
        sent(exists[direction], lambda: s_copy(direction))
        sent(exists[direction], lambda: c_copy(direction))
    for k in range(3):
        sent(always, lambda: f_copy(k))
        sent(always, lambda: t_copy(k))


def body(states, previous, potential, tile_atom, tile_cells, tile_count, projectors, coupling, rotation):
    vmem = pl.BlockSpec(memory_space=pltpu.VMEM)
    dma = pltpu.SemaphoreType.DMA
    operands = (
        states,
        previous,
        potential.reshape(1, -1),
        tile_atom.reshape(1, -1),
        tile_cells,
        projectors,
        coupling,
        rotation,
    )
    return pl.pallas_call(
        kernel,
        out_shape=jax.ShapeDtypeStruct((QUARTER, 128), F32),
        in_specs=[pl.BlockSpec(memory_space=pltpu.SMEM)] + [pl.BlockSpec(memory_space=pltpu.HBM)] * 8,
        out_specs=vmem,
        scratch_shapes=[
            *(pltpu.VMEM(operand.shape, operand.dtype) for operand in operands),
            dma((8,)),
            pltpu.VMEM((256, QUARTER), BF16),
            pltpu.VMEM((256, QUARTER), BF16),
            pltpu.VMEM((32, 4096), F32),
            pltpu.VMEM((2, 32, 4096), F32),
            pltpu.VMEM((32, QUARTER), F32),
            pltpu.VMEM((2, 32, 4096), F32),
            pltpu.VMEM((2, 32, 4096), F32),
            pltpu.VMEM((2, 32, 512), F32),
            pltpu.VMEM((2, 32, 512), F32),
            pltpu.VMEM((6, 8, 128), F32),
            pltpu.VMEM((6, 8, 128), F32),
            pltpu.VMEM((8, 128), F32),
            pltpu.VMEM((6, 8, 128), F32),
            pltpu.VMEM((3, 32, QUARTER), F32),
            pltpu.VMEM((8, 896), F32),
            pltpu.VMEM((3, 8, 896), F32),
            pltpu.VMEM((4, 128, 96), BF16),
            pltpu.VMEM((128, QUARTER), F32),
            pltpu.VMEM((512, 4096), BF16),
            pltpu.VMEM((512, 4096), BF16),
            pltpu.VMEM((224, 512), BF16),
            dma((7, 8)),
            dma((7, 8)),
            dma((2, 8)),
            dma((2, 8)),
            dma((2,)),
            dma((2,)),
            dma((6,)),
            dma((6,)),
            dma((6,)),
            dma((6,)),
            dma((3,)),
            dma((3,)),
            dma((3,)),
            dma((3,)),
            pltpu.SemaphoreType.REGULAR((2,)),
        ],
        compiler_params=pltpu.CompilerParams(
            collective_id=0, has_side_effects=True, vmem_limit_bytes=64 * 1024 * 1024
        ),
        name="chebyshev_step",
    )(tile_count, *operands)


def solution(mesh):
    placed = (
        P("band", "dom"),
        P("band", "dom"),
        P("dom"),
        P("dom"),
        P("dom", None),
        P("dom"),
        P("dom", None, None),
        P("dom", None, None),
        P(),
    )
    return jax.shard_map(
        body, mesh=mesh, in_specs=placed, out_specs=P(("dom", "band"), None), check_vma=False
    )
```
